32 devices in a mesh: arcs: 2 (over y), seg: 16 (over z, x, core).
Axes of the slice: x: 2, y: 2, z: 4, core: 2. Of those that a mesh axis runs over, the one named last changes fastest.
Arguments:
- pulses: bfloat16 [2, 8192, 256], P(None, ('arcs', 'seg')), parts along dimension 1, may hold values from -6 to 6
- fraction: float32 [8192], P(('arcs', 'seg')), parts along dimension 0, may hold values from 0 to 1
- gate_shift: int32 [8192], P(('arcs', 'seg')), parts along dimension 0, may hold values from 0 to 15
- aperture_start: int32 [4096], P(('arcs', 'seg')), parts along dimension 0, may hold values from 0 to 4095, as said below
- aperture_end: int32 [4096], P(('arcs', 'seg')), parts along dimension 0, may hold values from 257 to 4096, as said below
- doppler: float32 [4096], P(('arcs', 'seg')), parts along dimension 0, may hold values from -2000 to 2000
- chirp_rate: float32 [4096], P(('arcs', 'seg')), parts along dimension 0, may hold values from 2000 to 6000
Outputs:
- focused: bfloat16 [2, 4096, 256], P(None, ('arcs', 'seg')), parts along dimension 1
- multilook: float32 [4096, 256], P(('arcs', 'seg')), parts along dimension 0
The draws below stay inside these ranges and needn't reach their ends.
There are 2 independent parts, one for each index of `arcs`. The reference program is written for one: setup_inputs(seed, part) draws one part's arguments, and reference() takes and returns one part's arrays. A program takes and returns all parts, laid end to end along the dimension named above; each array names one. Nothing has to cross between parts.
Inputs may be any that keep to these rules, and one draw needn't show every extreme that they name: aperture_start[w] >= (w // 128 - 4) * 256, with equality for some waveform; aperture_end[w] - aperture_start[w] >= 257. aperture_end[w] <= (w // 128 + 5) * 256, with equality for some waveform; aperture_start[w] < aperture_end[w].
All inputs are finite; a program needn't handle non-finite values.
Results may differ from the reference program's by a relative error of at most 0.0064.
Values may be sent and summed in bfloat16 or wider, within the bound.
A program may use at most 64 MiB of HBM per device.

```python
import jax
import jax.numpy as jnp
from jax import lax

G = 256
P_DEV = 256
W_DEV = 128
REACH = 4
LOOK = 8
SHIFT_MAX = 16
PULSES = 4096
WAVES = 2048
N_SEG = 16


def aperture_pair(key):
    aperture_key = jax.random.fold_in(key, 7321)
    wave_index = jnp.arange(WAVES, dtype=jnp.int32)
    device = wave_index // W_DEV
    within = wave_index % W_DEV
    center = device * P_DEV + within * P_DEV // W_DEV + P_DEV // (2 * W_DEV)
    half_span = jax.random.randint(aperture_key, (WAVES,), P_DEV, REACH * P_DEV + 1, dtype=jnp.int32)
    first_mark = WAVES // 2
    second_mark = WAVES // 2 + W_DEV - 1
    half_span = jnp.where(wave_index == first_mark, REACH * P_DEV + P_DEV // (2 * W_DEV), half_span)
    reach_end = (device + REACH + 1) * P_DEV - 1 - center
    half_span = jnp.where(wave_index == second_mark, reach_end, half_span)
    first_pulse = jnp.maximum(center - half_span, 0)
    last_pulse = jnp.minimum(center + half_span + 1, PULSES)
    return (first_pulse.astype(jnp.int32), last_pulse.astype(jnp.int32))


def draw_aperture_start(key, part):
    return aperture_pair(key)[0]


def draw_aperture_end(key, part):
    return aperture_pair(key)[1]


def with_ends(drawn, rng, smallest, high):
    longest = drawn.shape.index(max(drawn.shape))
    spots = []
    for shift in (0, 1):
        where = [jax.random.randint(jax.random.fold_in(rng, axis), (), 0, length) for axis, length in enumerate(drawn.shape)]
        where[longest] = (where[longest] + shift) % drawn.shape[longest]
        spots.append(tuple(where))
    return drawn.at[spots[0]].set(smallest).at[spots[1]].set(high)


def levels(key, shape, pieces, low, largest):
    gain = 1.0
    for axis_at, parts in pieces:
        draws = jax.random.uniform(jax.random.fold_in(jax.random.fold_in(key, 6), axis_at), (parts,), jnp.float32, low / len(pieces), largest / len(pieces))
        gain = gain * jnp.repeat(jnp.exp(draws), shape[axis_at] // parts).reshape((-1,) + (1,) * (len(shape) - 1 - axis_at))
    return gain


def gaussian(rng, shape, spread, reach, cuts=(), held_as=jnp.bfloat16):
    gain = levels(rng, shape, cuts, -0.22, 0.18) if cuts else 1.0
    values = jax.random.normal(rng, shape, jnp.float32) * spread * gain
    return jnp.minimum(jnp.maximum(values, -reach), reach).astype(held_as)


def setup_inputs(seed: int = 0, part: int = 0) -> dict:
    keys = jax.random.split(jax.random.key(seed), 8)
    part_splits = jax.random.split(jax.random.fold_in(keys[7], part), 8)
    return {
        "pulses": gaussian(part_splits[0], (2, PULSES, G), 1.0, 6.0, ((1, 16),)),
        "fraction": jnp.clip(1.0 * jax.random.uniform(part_splits[1], (PULSES,), jnp.float32) ** levels(part_splits[1], (PULSES,), ((0, 16),), -0.2, 0.2), 0.0, 1.0),
        "gate_shift": with_ends(jax.random.randint(part_splits[2], (PULSES,), 0, SHIFT_MAX), jax.random.fold_in(part_splits[2], 1), 0, SHIFT_MAX - 1).astype(jnp.int32),
        "aperture_start": draw_aperture_start(jax.random.fold_in(jax.random.fold_in(keys[7], part), 71), part),
        "aperture_end": draw_aperture_end(jax.random.fold_in(jax.random.fold_in(keys[7], part), 71), part),
        "doppler": jnp.clip(jax.random.uniform(part_splits[5], (WAVES,), jnp.float32, -2000.0, 2000.0) * levels(part_splits[5], (WAVES,), ((0, 16),), -0.4, 0.0), -2000.0, 2000.0),
        "chirp_rate": jnp.clip(2000.0 + 4000.0 * jax.random.uniform(part_splits[6], (WAVES,), jnp.float32) ** levels(part_splits[6], (WAVES,), ((0, 16),), -0.2, 0.2), 2000.0, 6000.0),
    }


def migrate(pulses, fraction, gate_shift):
    widened = jnp.pad(pulses.astype(jnp.float32), ((0, 0), (0, 0), (0, SHIFT_MAX + 1)))
    blend = fraction[None, :, None]
    shift_col = gate_shift[None, :, None]
    result = jnp.zeros(pulses.shape, jnp.float32)
    for gate_step in range(SHIFT_MAX + 1):
        coeff = jnp.where(shift_col == gate_step, 1.0 - blend, 0.0) + jnp.where(shift_col + 1 == gate_step, blend, 0.0)
        result = result + coeff * widened[:, :, gate_step:gate_step + G]
    return result.astype(jnp.bfloat16)

def weights(first_pulse, last_pulse, doppler, chirp_rate, pulse_index):
    center = (first_pulse + last_pulse) // 2
    relative = (pulse_index[None, :] - center[:, None]).astype(jnp.float32) / float(REACH * P_DEV)
    phase_angle = chirp_rate[:, None] * relative * relative + doppler[:, None] * relative
    inside = (pulse_index[None, :] >= first_pulse[:, None]) & (pulse_index[None, :] < last_pulse[:, None])
    amplitude = lax.rsqrt((last_pulse - first_pulse).astype(jnp.float32))[:, None]
    weight_re = jnp.where(inside, amplitude * jnp.cos(phase_angle), 0.0).astype(jnp.bfloat16)
    weight_im = jnp.where(inside, amplitude * jnp.sin(phase_angle), 0.0).astype(jnp.bfloat16)
    return (weight_re, weight_im)

def focus_block(weight_re, weight_im, block_data):
    real_part = jnp.dot(weight_re, block_data[0], preferred_element_type=jnp.float32) - jnp.dot(weight_im, block_data[1], preferred_element_type=jnp.float32)
    imag_part = jnp.dot(weight_re, block_data[1], preferred_element_type=jnp.float32) + jnp.dot(weight_im, block_data[0], preferred_element_type=jnp.float32)
    return jnp.stack([real_part, imag_part])

def settle(term):
    rounded = lax.optimization_barrier(term.astype(jnp.bfloat16))
    return rounded.astype(jnp.float32)

def reference(pulses, fraction, gate_shift, aperture_start, aperture_end, doppler, chirp_rate):
    migrated = migrate(pulses, fraction, gate_shift)
    padded = jnp.pad(migrated, ((0, 0), (REACH * P_DEV, REACH * P_DEV), (0, 0)))
    window_len = (2 * REACH + 1) * P_DEV

    def one_block(block_index):
        window = lax.dynamic_slice_in_dim(padded, block_index * P_DEV, window_len, 1)
        pulse_index = (block_index - REACH) * P_DEV + jnp.arange(window_len, dtype=jnp.int32)
        first_pulse = lax.dynamic_slice_in_dim(aperture_start, block_index * W_DEV, W_DEV)
        last_pulse = lax.dynamic_slice_in_dim(aperture_end, block_index * W_DEV, W_DEV)
        rate_one = lax.dynamic_slice_in_dim(doppler, block_index * W_DEV, W_DEV)
        rate_two = lax.dynamic_slice_in_dim(chirp_rate, block_index * W_DEV, W_DEV)
        weight_re, weight_im = weights(first_pulse, last_pulse, rate_one, rate_two, pulse_index)
        total = jnp.zeros((2, W_DEV, G), jnp.float32)
        for block_slot in range(2 * REACH + 1):
            low = block_slot * P_DEV
            term = focus_block(weight_re[:, low:low + P_DEV], weight_im[:, low:low + P_DEV], window[:, low:low + P_DEV])
            total = total + settle(term)
        return total
    blocks = lax.map(one_block, jnp.arange(N_SEG, dtype=jnp.int32))
    focused_sum = jnp.transpose(blocks, (1, 0, 2, 3)).reshape(2, WAVES, G)
    power_sum = focused_sum[0] * focused_sum[0] + focused_sum[1] * focused_sum[1]
    power_pad = jnp.pad(power_sum, ((LOOK, LOOK), (0, 0)))
    looked = jnp.zeros((WAVES, G), jnp.float32)
    for shift_row in range(2 * LOOK + 1):
        looked = looked + power_pad[shift_row:shift_row + WAVES]
    multilook = looked / float(2 * LOOK + 1)
    return (focused_sum.astype(jnp.bfloat16), multilook)
```

```python
import functools
import math

import jax
import jax.numpy as jnp
from jax import lax
from jax.experimental import pallas as pl
from jax.experimental.pallas import tpu as pltpu
from jax.sharding import PartitionSpec as P

REACH = 4
LOOK = 8
SHIFT_BITS = 4
ROWS = 32
MESH = pl.DeviceIdType.MESH

SIN = (3.141592640130708, -5.167710083507871, 2.550077523214076, -0.5982912856170641, 0.07765766029898877)
COS = (0.9999999532476084, -4.93479283061964, 4.058411352862407, -1.3318765680796267, 0.21968961109548557)


def horner(coefs, u):
    result = coefs[-1] * u + coefs[-2]
    for c in coefs[-3::-1]:
        result = result * u + c
    return result


def kernel(n, pulses_ref, gates_ref, params_ref, focus_ref, look_ref,
           mig, wts, cols, gcols, pbuf, sendb, recvb, acc, power,
           psend, precv, tsend, trecv, hsend, hrecv):
    me = lax.axis_index("seg")
    pulse_count, gates = pulses_ref.shape[1:]
    waves = params_ref.shape[1]
    scale = 1.0 / float(REACH * pulse_count)
    slots = 2 * REACH

    def offset(i):
        mag = REACH - lax.div(i, 2)
        return mag * (1 - 2 * lax.rem(i, 2))

    def exists(d):
        return (d >= 0) & (d < n)

    def each(body):
        def step(i, carry):
            body(i, offset(i))
            return carry
        lax.fori_loop(0, slots, step, 0)

    barrier = pltpu.get_barrier_semaphore()

    def greet(i, o):
        @pl.when(exists(me + o))
        def _():
            pl.semaphore_signal(barrier, inc=1, device_id={"seg": me + o}, device_id_type=MESH)

    each(greet)
    gcols[...] = gates_ref[...].T
    lane = lax.broadcasted_iota(jnp.int32, (ROWS, gates), 1)

    def migrate_rows(q, carry):
        rows = pl.ds(pl.multiple_of(q * ROWS, ROWS), ROWS)
        frac = gcols[rows, 0:1]
        shift = gcols[rows, 1:2].astype(jnp.int32)
        for c in range(2):
            x = pulses_ref[c, rows, :].astype(jnp.float32)
            nxt = jnp.where(lane == gates - 1, 0.0, pltpu.roll(x, gates - 1, 1))
            z = (1.0 - frac) * x + frac * nxt
            for b in range(SHIFT_BITS):
                z = jnp.where((shift & (1 << b)) != 0, pltpu.roll(z, gates - (1 << b), 1), z)
            z = jnp.where(lane + shift < gates, z, 0.0)
            mig[rows, c * gates:(c + 1) * gates] = z.astype(jnp.bfloat16)
        return carry

    pl.semaphore_wait(barrier, jnp.minimum(me, REACH) + jnp.minimum(n - 1 - me, REACH))

    def params_copy(i, target):
        return pltpu.make_async_remote_copy(
            src_ref=params_ref, dst_ref=pbuf.at[i], send_sem=psend.at[i], recv_sem=precv.at[i],
            device_id={"seg": target}, device_id_type=MESH)

    def send_params(i, o):
        @pl.when(exists(me - o))
        def _():
            params_copy(i, me - o).start()

    each(send_params)
    lax.fori_loop(0, pulse_count // ROWS, migrate_rows, 0)

    pulse = (me * pulse_count + lax.broadcasted_iota(jnp.int32, (ROWS, pulse_count), 1)).astype(jnp.float32)

    def term(packed):
        cols[...] = packed.T

        def weigh(q, carry):
            rows = pl.ds(pl.multiple_of(q * ROWS, ROWS), ROWS)
            low = pl.ds(pl.multiple_of(waves + q * ROWS, ROWS), ROWS)
            center, start, end = cols[rows, 0:1], cols[rows, 1:2], cols[rows, 2:3]
            rate, slope, amp = cols[rows, 3:4], cols[rows, 4:5], cols[rows, 5:6]
            r = (pulse - center) * scale
            t = r * (rate * r + slope)
            t = t - jnp.floor(t + 0.5)
            u = t * t
            s = t * horner(SIN, u)
            c = horner(COS, u)
            a = jnp.where((pulse >= start) & (pulse < end), amp, 0.0)
            twice = (a + a) * s
            wts[rows, :] = (a - twice * s).astype(jnp.bfloat16)
            wts[low, :] = (twice * c).astype(jnp.bfloat16)
            return carry

        lax.fori_loop(0, waves // ROWS, weigh, 0)
        real = jnp.dot(wts[...], mig[:, :gates], preferred_element_type=jnp.float32)
        imag = jnp.dot(wts[...], mig[:, gates:], preferred_element_type=jnp.float32)
        return real[:waves] - imag[waves:], imag[:waves] + real[waves:]

    def term_copy(i, target):
        return pltpu.make_async_remote_copy(
            src_ref=sendb.at[i], dst_ref=recvb.at[i], send_sem=tsend.at[i], recv_sem=trecv.at[i],
            device_id={"seg": target}, device_id_type=MESH)

    def send_term(i, o):
        @pl.when(exists(me + o))
        def _():
            params_copy(i, me + o).wait_recv()
            real, imag = term(pbuf[i])
            sendb[i, 0] = real.astype(jnp.bfloat16)
            sendb[i, 1] = imag.astype(jnp.bfloat16)
            term_copy(i, me + o).start()

    each(send_term)
    real, imag = term(params_ref[...])
    acc[0] = real
    acc[1] = imag

    def take(j, o):
        i = slots - 1 - j
        o = offset(i)

        @pl.when(exists(me - o))
        def _():
            term_copy(i, me - o).wait_recv()
            acc[0] += recvb[i, 0].astype(jnp.float32)
            acc[1] += recvb[i, 1].astype(jnp.float32)

    each(take)
    power[LOOK:LOOK + waves, :] = acc[0] * acc[0] + acc[1] * acc[1]

    def halo_copy(side):
        low = LOOK if side == 0 else waves
        into = LOOK + waves if side == 0 else 0
        target = me - 1 if side == 0 else me + 1
        return pltpu.make_async_remote_copy(
            src_ref=power.at[pl.ds(low, LOOK)], dst_ref=power.at[pl.ds(into, LOOK)],
            send_sem=hsend.at[side], recv_sem=hrecv.at[side],
            device_id={"seg": target}, device_id_type=MESH)

    @pl.when(me > 0)
    def _():
        halo_copy(0).start()

    @pl.when(me < n - 1)
    def _():
        halo_copy(1).start()

    @pl.when(me == 0)
    def _():
        power[0:LOOK, :] = jnp.zeros((LOOK, gates), jnp.float32)

    @pl.when(me == n - 1)
    def _():
        power[LOOK + waves:, :] = jnp.zeros((LOOK, gates), jnp.float32)

    focus_ref[...] = acc[...].astype(jnp.bfloat16)

    def drain(i, o):
        @pl.when(exists(me - o))
        def _():
            params_copy(i, me - o).wait_send()

        @pl.when(exists(me + o))
        def _():
            term_copy(i, me + o).wait_send()

    each(drain)

    @pl.when(me > 0)
    def _():
        halo_copy(0).wait_send()
        halo_copy(1).wait_recv()

    @pl.when(me < n - 1)
    def _():
        halo_copy(1).wait_send()
        halo_copy(0).wait_recv()

    total = power[...]
    size = waves + 2 * LOOK
    last = total[2 * LOOK:]
    step = 1
    while step < 2 * LOOK:
        size -= step
        total = total[:size] + total[step:step + size]
        step *= 2
    look_ref[...] = (total[:waves] + last) * (1.0 / float(2 * LOOK + 1))


def shards(pulses, fraction, gate_shift, aperture_start, aperture_end, doppler, chirp_rate):
    n = lax.axis_size("seg")
    pulse_count, gates = pulses.shape[1:]
    waves = aperture_start.shape[0]
    f32 = jnp.float32
    turn = 1.0 / (2.0 * math.pi)
    start, end = aperture_start, aperture_end
    none = jnp.zeros((waves,), f32)
    params = jnp.stack([
        ((start + end) // 2).astype(f32), start.astype(f32), end.astype(f32),
        chirp_rate * turn, doppler * turn, lax.rsqrt((end - start).astype(f32)), none, none])
    blank = jnp.zeros((pulse_count,), f32)
    packed = jnp.stack([fraction, gate_shift.astype(f32)] + [blank] * 6)
    vmem = pl.BlockSpec(memory_space=pltpu.VMEM)
    slots = 2 * REACH
    dma = pltpu.SemaphoreType.DMA
    return pl.pallas_call(
        functools.partial(kernel, n),
        out_shape=(jax.ShapeDtypeStruct((2, waves, gates), jnp.bfloat16),
                   jax.ShapeDtypeStruct((waves, gates), f32)),
        in_specs=[vmem] * 3,
        out_specs=(vmem, vmem),
        scratch_shapes=[
            pltpu.VMEM((pulse_count, 2 * gates), jnp.bfloat16),
            pltpu.VMEM((2 * waves, pulse_count), jnp.bfloat16),
            pltpu.VMEM((waves, 8), f32),
            pltpu.VMEM((pulse_count, 8), f32),
            pltpu.VMEM((slots, 8, waves), f32),
            pltpu.VMEM((slots, 2, waves, gates), jnp.bfloat16),
            pltpu.VMEM((slots, 2, waves, gates), jnp.bfloat16),
            pltpu.VMEM((2, waves, gates), f32),
            pltpu.VMEM((waves + 2 * LOOK, gates), f32),
            dma((slots,)), dma((slots,)), dma((slots,)), dma((slots,)), dma((2,)), dma((2,)),
        ],
        compiler_params=pltpu.CompilerParams(
            collective_id=0, has_side_effects=True, vmem_limit_bytes=16 * 1024 * 1024),
    )(pulses, packed, params)


def solution(mesh):
    seg = P(("arcs", "seg"))
    return jax.shard_map(
        shards,
        mesh=mesh,
        in_specs=(P(None, ("arcs", "seg"), None), seg, seg, seg, seg, seg, seg),
        out_specs=(P(None, ("arcs", "seg"), None), P(("arcs", "seg"), None)),
        check_vma=False,
    )
```

```python
import functools
import math

import jax
import jax.numpy as jnp
from jax import lax
from jax.experimental import pallas as pl
from jax.experimental.pallas import tpu as pltpu
from jax.sharding import PartitionSpec as P

REACH = 4
LOOK = 8
SHIFT_BITS = 4
ROWS = 32
MESH = pl.DeviceIdType.MESH

SIN = (3.141592640130708, -5.167710083507871, 2.550077523214076, -0.5982912856170641, 0.07765766029898877)
COS = (0.9999999532476084, -4.93479283061964, 4.058411352862407, -1.3318765680796267, 0.21968961109548557)


def horner(coefs, u):
    result = coefs[-1] * u + coefs[-2]
    for c in coefs[-3::-1]:
        result = result * u + c
    return result


def kernel(n, pulses_hbm, fraction_hbm, shift_hbm, start_hbm, end_hbm, doppler_hbm, chirp_hbm,
           focus_ref, look_ref,
           pulses_ref, fraction_ref, shift_ref, start_ref, end_ref, doppler_ref, chirp_ref,
           params_ref, gates_ref, mig, wts, cols, gcols, pbuf, helpb, gotb, sendb, recvb, acc, power,
           insem, psend, precv, gsend, grecv, tsend, trecv, hsend, hrecv):
    me = lax.axis_index("seg")
    core = lax.rem(me, 2)
    way = 1 - 2 * core
    mate = me + way
    pulse_count, gates = pulses_ref.shape[1:]
    waves = params_ref.shape[1]
    scale = 1.0 / float(REACH * pulse_count)

    def exists(d):
        return (d >= 0) & (d < n)

    def loop(count, body):
        def step(i, carry):
            body(i)
            return carry
        lax.fori_loop(0, count, step, 0)

    def each(body):
        def peer(i):
            @pl.when((i != REACH) & exists(me + i - REACH))
            def _():
                body(i, me + i - REACH)
        loop(2 * REACH + 1, peer)

    barrier = pltpu.get_barrier_semaphore()

    def greet(i, peer):
        pl.semaphore_signal(barrier, inc=1, device_id={"seg": peer}, device_id_type=MESH)

    each(greet)
    loads = [pltpu.make_async_copy(src, dst, insem.at[i]) for i, (src, dst) in enumerate((
        (start_hbm, start_ref), (end_hbm, end_ref), (doppler_hbm, doppler_ref), (chirp_hbm, chirp_ref),
        (fraction_hbm, fraction_ref), (shift_hbm, shift_ref), (pulses_hbm, pulses_ref)))]
    for load in loads:
        load.start()
    for load in loads[:4]:
        load.wait()
    start, end = start_ref[...], end_ref[...]
    f32 = jnp.float32
    turn = 1.0 / (2.0 * math.pi)
    params_ref[0:1, :] = lax.shift_right_arithmetic(start + end, 1).astype(f32)
    params_ref[1:2, :] = start.astype(f32)
    params_ref[2:3, :] = end.astype(f32)
    params_ref[3:4, :] = chirp_ref[...] * turn
    params_ref[4:5, :] = doppler_ref[...] * turn
    params_ref[5:6, :] = lax.rsqrt((end - start).astype(f32))
    params_ref[6:8, :] = jnp.zeros((2, waves), f32)
    pl.semaphore_wait(barrier, jnp.minimum(me, REACH) + jnp.minimum(n - 1 - me, REACH))

    def params_copy(i, target):
        return pltpu.make_async_remote_copy(
            src_ref=params_ref, dst_ref=pbuf.at[i], send_sem=psend.at[i], recv_sem=precv.at[i],
            device_id={"seg": target}, device_id_type=MESH)

    each(lambda i, peer: params_copy(2 * REACH - i, peer).start())
    for load in loads[4:]:
        load.wait()
    gates_ref[0:1, :] = fraction_ref[...]
    gates_ref[1:2, :] = shift_ref[...].astype(f32)
    gates_ref[2:8, :] = jnp.zeros((6, pulse_count), f32)
    gcols[...] = gates_ref[...].T
    lane = lax.broadcasted_iota(jnp.int32, (ROWS, gates), 1)

    def migrate_rows(q, carry):
        rows = pl.ds(pl.multiple_of(q * ROWS, ROWS), ROWS)
        frac = gcols[rows, 0:1]
        shift = gcols[rows, 1:2].astype(jnp.int32)
        for c in range(2):
            x = pulses_ref[c, rows, :].astype(jnp.float32)
            nxt = jnp.where(lane == gates - 1, 0.0, pltpu.roll(x, gates - 1, 1))
            z = (1.0 - frac) * x + frac * nxt
            for b in range(SHIFT_BITS):
                z = jnp.where((shift & (1 << b)) != 0, pltpu.roll(z, gates - (1 << b), 1), z)
            z = jnp.where(lane + shift < gates, z, 0.0)
            mig[rows, c * gates:(c + 1) * gates] = z.astype(jnp.bfloat16)
        return carry

    lax.fori_loop(0, pulse_count // ROWS, migrate_rows, 0)

    pulse = (me * pulse_count + lax.broadcasted_iota(jnp.int32, (ROWS, pulse_count), 1)).astype(jnp.float32)

    def term(packed):
        cols[...] = packed.T

        def weigh(q, carry):
            rows = pl.ds(pl.multiple_of(q * ROWS, ROWS), ROWS)
            low = pl.ds(pl.multiple_of(waves + q * ROWS, ROWS), ROWS)
            center, start, end = cols[rows, 0:1], cols[rows, 1:2], cols[rows, 2:3]
            rate, slope, amp = cols[rows, 3:4], cols[rows, 4:5], cols[rows, 5:6]
            r = (pulse - center) * scale
            t = r * (rate * r + slope)
            t = t - jnp.floor(t + 0.5)
            u = t * t
            s = t * horner(SIN, u)
            c = horner(COS, u)
            a = jnp.where((pulse >= start) & (pulse < end), amp, 0.0)
            twice = (a + a) * s
            wts[rows, :] = (a - twice * s).astype(jnp.bfloat16)
            wts[low, :] = (twice * c).astype(jnp.bfloat16)
            return carry

        lax.fori_loop(0, waves // ROWS, weigh, 0)
        real = jnp.dot(wts[...], mig[:, :gates], preferred_element_type=jnp.float32)
        imag = jnp.dot(wts[...], mig[:, gates:], preferred_element_type=jnp.float32)
        return real[:waves] - imag[waves:], imag[:waves] + real[waves:]

    def term_for(o):
        i = o + REACH
        params_copy(i, me + o).wait_recv()
        return term(pbuf[i])

    def own(k):
        return 4 - 2 * k - 2 * lax.div(k, 2)

    def help_copy(k):
        return pltpu.make_async_remote_copy(
            src_ref=helpb.at[k], dst_ref=gotb.at[k], send_sem=gsend.at[k], recv_sem=grecv.at[k],
            device_id={"seg": mate}, device_id_type=MESH)

    def sum_copy(k, target):
        return pltpu.make_async_remote_copy(
            src_ref=sendb.at[k], dst_ref=recvb.at[k], send_sem=tsend.at[k], recv_sem=trecv.at[k],
            device_id={"seg": target}, device_id_type=MESH)

    def alone(k):
        @pl.when(exists(me + way * own(k)))
        def _():
            real, imag = term_for(way * own(k))
            sendb[k, 0] = real.astype(jnp.bfloat16)
            sendb[k, 1] = imag.astype(jnp.bfloat16)
            sum_copy(k, me + way * own(k)).start()

    def assist(k):
        o = way * (1 - own(k))

        @pl.when(exists(me + o))
        def _():
            real, imag = term_for(o)
            helpb[k, 0] = real.astype(jnp.bfloat16)
            helpb[k, 1] = imag.astype(jnp.bfloat16)
            help_copy(k).start()

    def shared(k):
        @pl.when(exists(me + way * own(k)))
        def _():
            real, imag = term_for(way * own(k))
            help_copy(k).wait_recv()
            sendb[k, 0] = (real + gotb[k, 0].astype(f32)).astype(jnp.bfloat16)
            sendb[k, 1] = (imag + gotb[k, 1].astype(f32)).astype(jnp.bfloat16)
            sum_copy(k, me + way * own(k)).start()

    loop(1, lambda k: alone(k + 3))
    loop(3, assist)
    loop(3, shared)
    real, imag = term_for(way)
    helpb[3, 0] = real.astype(jnp.bfloat16)
    helpb[3, 1] = imag.astype(jnp.bfloat16)
    help_copy(3).start()
    real, imag = term(params_ref[...])
    help_copy(3).wait_recv()
    acc[0] = real + gotb[3, 0].astype(f32)
    acc[1] = imag + gotb[3, 1].astype(f32)

    def take(j):
        k = 3 - j

        @pl.when(exists(me - way * own(k)))
        def _():
            sum_copy(k, me - way * own(k)).wait_recv()
            acc[0] += recvb[k, 0].astype(f32)
            acc[1] += recvb[k, 1].astype(f32)

    loop(4, take)
    power[LOOK:LOOK + waves, :] = acc[0] * acc[0] + acc[1] * acc[1]

    def halo_copy(side):
        low = LOOK if side == 0 else waves
        into = LOOK + waves if side == 0 else 0
        target = me - 1 if side == 0 else me + 1
        return pltpu.make_async_remote_copy(
            src_ref=power.at[pl.ds(low, LOOK)], dst_ref=power.at[pl.ds(into, LOOK)],
            send_sem=hsend.at[side], recv_sem=hrecv.at[side],
            device_id={"seg": target}, device_id_type=MESH)

    @pl.when(me > 0)
    def _():
        halo_copy(0).start()

    @pl.when(me < n - 1)
    def _():
        halo_copy(1).start()

    @pl.when(me == 0)
    def _():
        power[0:LOOK, :] = jnp.zeros((LOOK, gates), jnp.float32)

    @pl.when(me == n - 1)
    def _():
        power[LOOK + waves:, :] = jnp.zeros((LOOK, gates), jnp.float32)

    focus_ref[...] = acc[...].astype(jnp.bfloat16)

    each(lambda i, peer: params_copy(2 * REACH - i, peer).wait_send())

    def drain(k):
        @pl.when(exists(me + way * own(k)))
        def _():
            sum_copy(k, me + way * own(k)).wait_send()

    loop(4, drain)

    def drain_help(k):
        @pl.when(exists(me + way * (1 - own(k))))
        def _():
            help_copy(k).wait_send()

    loop(3, drain_help)
    help_copy(3).wait_send()

    @pl.when(me > 0)
    def _():
        halo_copy(0).wait_send()
        halo_copy(1).wait_recv()

    @pl.when(me < n - 1)
    def _():
        halo_copy(1).wait_send()
        halo_copy(0).wait_recv()

    total = power[...]
    size = waves + 2 * LOOK
    last = total[2 * LOOK:]
    step = 1
    while step < 2 * LOOK:
        size -= step
        total = total[:size] + total[step:step + size]
        step *= 2
    look_ref[...] = (total[:waves] + last) * (1.0 / float(2 * LOOK + 1))


def shards(pulses, fraction, gate_shift, aperture_start, aperture_end, doppler, chirp_rate):
    n = lax.axis_size("seg")
    pulse_count, gates = pulses.shape[1:]
    waves = aperture_start.shape[0]
    f32 = jnp.float32
    vmem = pl.BlockSpec(memory_space=pltpu.VMEM)
    hbm = pl.BlockSpec(memory_space=pltpu.HBM)
    slots = 2 * REACH + 1
    dma = pltpu.SemaphoreType.DMA
    block = pltpu.VMEM((4, 2, waves, gates), jnp.bfloat16)
    rows = [a.reshape(1, -1) for a in (
        fraction, gate_shift, aperture_start, aperture_end, doppler, chirp_rate)]
    return pl.pallas_call(
        functools.partial(kernel, n),
        out_shape=(jax.ShapeDtypeStruct((2, waves, gates), jnp.bfloat16),
                   jax.ShapeDtypeStruct((waves, gates), f32)),
        in_specs=[hbm] * 7,
        out_specs=(vmem, vmem),
        scratch_shapes=[pltpu.VMEM(pulses.shape, pulses.dtype)] + [pltpu.VMEM(a.shape, a.dtype) for a in rows] + [
            pltpu.VMEM((8, waves), f32),
            pltpu.VMEM((8, pulse_count), f32),
            pltpu.VMEM((pulse_count, 2 * gates), jnp.bfloat16),
            pltpu.VMEM((2 * waves, pulse_count), jnp.bfloat16),
            pltpu.VMEM((waves, 8), f32),
            pltpu.VMEM((pulse_count, 8), f32),
            pltpu.VMEM((slots, 8, waves), f32),
            block, block, block, block,
            pltpu.VMEM((2, waves, gates), f32),
            pltpu.VMEM((waves + 2 * LOOK, gates), f32),
            dma((7,)), dma((slots,)), dma((slots,)), dma((4,)), dma((4,)), dma((4,)), dma((4,)), dma((2,)), dma((2,)),
        ],
        compiler_params=pltpu.CompilerParams(
            collective_id=0, has_side_effects=True, vmem_limit_bytes=60 * 1024 * 1024),
    )(pulses, *rows)


def solution(mesh):
    seg = P(("arcs", "seg"))
    return jax.shard_map(
        shards,
        mesh=mesh,
        in_specs=(P(None, ("arcs", "seg"), None), seg, seg, seg, seg, seg, seg),
        out_specs=(P(None, ("arcs", "seg"), None), P(("arcs", "seg"), None)),
        check_vma=False,
    )
```

```python
import functools
import math

import jax
import jax.numpy as jnp
from jax import lax
from jax.experimental import pallas as pl
from jax.experimental.pallas import tpu as pltpu
from jax.sharding import PartitionSpec as P

REACH = 4
LOOK = 8
SHIFT_BITS = 4
ROWS = 32
MESH = pl.DeviceIdType.MESH

SIN = (3.141592640130708, -5.167710083507871, 2.550077523214076, -0.5982912856170641, 0.07765766029898877)
COS = (0.9999999532476084, -4.93479283061964, 4.058411352862407, -1.3318765680796267, 0.21968961109548557)


def horner(coefs, u):
    result = coefs[-1] * u + coefs[-2]
    for c in coefs[-3::-1]:
        result = result * u + c
    return result


def kernel(n, pulses_hbm, fraction_hbm, shift_hbm, start_hbm, end_hbm, doppler_hbm, chirp_hbm,
           focus_ref, look_ref,
           pulses_ref, fraction_ref, shift_ref, start_ref, end_ref, doppler_ref, chirp_ref,
           params_ref, gates_ref, mig, wts, cols, gcols, pbuf, helpb, gotb, sendb, recvb, acc, power,
           insem, psend, precv, gsend, grecv, tsend, trecv, hsend, hrecv):
    me = lax.axis_index("seg")
    core = lax.rem(me, 2)
    way = 1 - 2 * core
    mate = me + way
    pulse_count, gates = pulses_ref.shape[1:]
    waves = params_ref.shape[1]
    scale = 1.0 / float(REACH * pulse_count)

    def exists(d):
        return (d >= 0) & (d < n)

    def loop(count, body):
        def step(i, carry):
            body(i)
            return carry
        lax.fori_loop(0, count, step, 0)

    def each(body):
        def peer(i):
            @pl.when((i != REACH) & exists(me + i - REACH))
            def _():
                body(i, me + i - REACH)
        loop(2 * REACH + 1, peer)

    barrier = pltpu.get_barrier_semaphore()

    def greet(i, peer):
        pl.semaphore_signal(barrier, inc=1, device_id={"seg": peer}, device_id_type=MESH)

    each(greet)
    loads = [pltpu.make_async_copy(src, dst, insem.at[i]) for i, (src, dst) in enumerate((
        (start_hbm, start_ref), (end_hbm, end_ref), (doppler_hbm, doppler_ref), (chirp_hbm, chirp_ref),
        (fraction_hbm, fraction_ref), (shift_hbm, shift_ref), (pulses_hbm, pulses_ref)))]
    for load in loads:
        load.start()
    for load in loads[:4]:
        load.wait()
    start, end = start_ref[...], end_ref[...]
    f32 = jnp.float32
    turn = 1.0 / (2.0 * math.pi)
    params_ref[0:1, :] = lax.shift_right_arithmetic(start + end, 1).astype(f32)
    params_ref[1:2, :] = start.astype(f32)
    params_ref[2:3, :] = end.astype(f32)
    params_ref[3:4, :] = chirp_ref[...] * turn
    params_ref[4:5, :] = doppler_ref[...] * turn
    params_ref[5:6, :] = lax.rsqrt((end - start).astype(f32))
    params_ref[6:8, :] = jnp.zeros((2, waves), f32)
    pl.semaphore_wait(barrier, jnp.minimum(me, REACH) + jnp.minimum(n - 1 - me, REACH))

    def params_copy(i, target):
        return pltpu.make_async_remote_copy(
            src_ref=params_ref, dst_ref=pbuf.at[i], send_sem=psend.at[i], recv_sem=precv.at[i],
            device_id={"seg": target}, device_id_type=MESH)

    each(lambda i, peer: params_copy(2 * REACH - i, peer).start())
    for load in loads[4:]:
        load.wait()
    gates_ref[0:1, :] = fraction_ref[...]
    gates_ref[1:2, :] = shift_ref[...].astype(f32)
    gates_ref[2:8, :] = jnp.zeros((6, pulse_count), f32)
    gcols[...] = gates_ref[...].T
    lane = lax.broadcasted_iota(jnp.int32, (ROWS, gates), 1)

    def migrate_rows(q, carry):
        rows = pl.ds(pl.multiple_of(q * ROWS, ROWS), ROWS)
        frac = gcols[rows, 0:1]
        shift = gcols[rows, 1:2].astype(jnp.int32)
        for c in range(2):
            x = pulses_ref[c, rows, :].astype(jnp.float32)
            nxt = jnp.where(lane == gates - 1, 0.0, pltpu.roll(x, gates - 1, 1))
            z = (1.0 - frac) * x + frac * nxt
            for b in range(SHIFT_BITS):
                z = jnp.where((shift & (1 << b)) != 0, pltpu.roll(z, gates - (1 << b), 1), z)
            z = jnp.where(lane + shift < gates, z, 0.0)
            mig[rows, c * gates:(c + 1) * gates] = z.astype(jnp.bfloat16)
        return carry

    lax.fori_loop(0, pulse_count // ROWS, migrate_rows, 0, unroll=4)

    pulse = (me * pulse_count + lax.broadcasted_iota(jnp.int32, (ROWS, pulse_count), 1)).astype(jnp.float32)

    def term(packed):
        cols[...] = packed.T

        def weigh(q, carry):
            rows = pl.ds(pl.multiple_of(q * ROWS, ROWS), ROWS)
            low = pl.ds(pl.multiple_of(waves + q * ROWS, ROWS), ROWS)
            center, start, end = cols[rows, 0:1], cols[rows, 1:2], cols[rows, 2:3]
            rate, slope, amp = cols[rows, 3:4], cols[rows, 4:5], cols[rows, 5:6]
            r = (pulse - center) * scale
            t = r * (rate * r + slope)
            t = t - jnp.floor(t + 0.5)
            u = t * t
            s = t * horner(SIN, u)
            c = horner(COS, u)
            a = jnp.where((pulse >= start) & (pulse < end), amp, 0.0)
            twice = (a + a) * s
            wts[rows, :] = (a - twice * s).astype(jnp.bfloat16)
            wts[low, :] = (twice * c).astype(jnp.bfloat16)
            return carry

        lax.fori_loop(0, waves // ROWS, weigh, 0, unroll=True)
        real = jnp.dot(wts[...], mig[:, :gates], preferred_element_type=jnp.float32)
        imag = jnp.dot(wts[...], mig[:, gates:], preferred_element_type=jnp.float32)
        return real[:waves] - imag[waves:], imag[:waves] + real[waves:]

    def term_for(o):
        i = o + REACH
        params_copy(i, me + o).wait_recv()
        return term(pbuf[i])

    def own(k):
        return 4 - 2 * k - 2 * lax.div(k, 2)

    def help_copy(k):
        return pltpu.make_async_remote_copy(
            src_ref=helpb.at[k], dst_ref=gotb.at[k], send_sem=gsend.at[k], recv_sem=grecv.at[k],
            device_id={"seg": mate}, device_id_type=MESH)

    def sum_copy(k, target):
        return pltpu.make_async_remote_copy(
            src_ref=sendb.at[k], dst_ref=recvb.at[k], send_sem=tsend.at[k], recv_sem=trecv.at[k],
            device_id={"seg": target}, device_id_type=MESH)

    def alone(k):
        @pl.when(exists(me + way * own(k)))
        def _():
            real, imag = term_for(way * own(k))
            sendb[k, 0] = real.astype(jnp.bfloat16)
            sendb[k, 1] = imag.astype(jnp.bfloat16)
            sum_copy(k, me + way * own(k)).start()

    def assist(k):
        o = way * (1 - own(k))

        @pl.when(exists(me + o))
        def _():
            real, imag = term_for(o)
            helpb[k, 0] = real.astype(jnp.bfloat16)
            helpb[k, 1] = imag.astype(jnp.bfloat16)
            help_copy(k).start()

    def shared(k):
        @pl.when(exists(me + way * own(k)))
        def _():
            real, imag = term_for(way * own(k))
            help_copy(k).wait_recv()
            sendb[k, 0] = (real + gotb[k, 0].astype(f32)).astype(jnp.bfloat16)
            sendb[k, 1] = (imag + gotb[k, 1].astype(f32)).astype(jnp.bfloat16)
            sum_copy(k, me + way * own(k)).start()

    loop(1, lambda k: alone(k + 3))
    loop(3, assist)
    loop(3, shared)
    real, imag = term_for(way)
    helpb[3, 0] = real.astype(jnp.bfloat16)
    helpb[3, 1] = imag.astype(jnp.bfloat16)
    help_copy(3).start()
    real, imag = term(params_ref[...])
    help_copy(3).wait_recv()
    acc[0] = real + gotb[3, 0].astype(f32)
    acc[1] = imag + gotb[3, 1].astype(f32)

    def take(j):
        k = 3 - j

        @pl.when(exists(me - way * own(k)))
        def _():
            sum_copy(k, me - way * own(k)).wait_recv()
            acc[0] += recvb[k, 0].astype(f32)
            acc[1] += recvb[k, 1].astype(f32)

    loop(4, take)
    power[LOOK:LOOK + waves, :] = acc[0] * acc[0] + acc[1] * acc[1]

    def halo_copy(side):
        low = LOOK if side == 0 else waves
        into = LOOK + waves if side == 0 else 0
        target = me - 1 if side == 0 else me + 1
        return pltpu.make_async_remote_copy(
            src_ref=power.at[pl.ds(low, LOOK)], dst_ref=power.at[pl.ds(into, LOOK)],
            send_sem=hsend.at[side], recv_sem=hrecv.at[side],
            device_id={"seg": target}, device_id_type=MESH)

    @pl.when(me > 0)
    def _():
        halo_copy(0).start()

    @pl.when(me < n - 1)
    def _():
        halo_copy(1).start()

    @pl.when(me == 0)
    def _():
        power[0:LOOK, :] = jnp.zeros((LOOK, gates), jnp.float32)

    @pl.when(me == n - 1)
    def _():
        power[LOOK + waves:, :] = jnp.zeros((LOOK, gates), jnp.float32)

    focus_ref[...] = acc[...].astype(jnp.bfloat16)

    def average(low, count):
        size = count + 2 * LOOK
        total = power[low:low + size, :]
        last = total[2 * LOOK:]
        step = 1
        while step < 2 * LOOK:
            size -= step
            total = total[:size] + total[step:step + size]
            step *= 2
        look_ref[low:low + count, :] = (total[:count] + last) * (1.0 / float(2 * LOOK + 1))

    average(LOOK, waves - 2 * LOOK)
    each(lambda i, peer: params_copy(2 * REACH - i, peer).wait_send())

    def drain(k):
        @pl.when(exists(me + way * own(k)))
        def _():
            sum_copy(k, me + way * own(k)).wait_send()

    loop(4, drain)

    def drain_help(k):
        @pl.when(exists(me + way * (1 - own(k))))
        def _():
            help_copy(k).wait_send()

    loop(3, drain_help)
    help_copy(3).wait_send()

    @pl.when(me > 0)
    def _():
        halo_copy(0).wait_send()
        halo_copy(1).wait_recv()

    @pl.when(me < n - 1)
    def _():
        halo_copy(1).wait_send()
        halo_copy(0).wait_recv()

    average(0, LOOK)
    average(waves - LOOK, LOOK)


def shards(pulses, fraction, gate_shift, aperture_start, aperture_end, doppler, chirp_rate):
    n = lax.axis_size("seg")
    pulse_count, gates = pulses.shape[1:]
    waves = aperture_start.shape[0]
    f32 = jnp.float32
    vmem = pl.BlockSpec(memory_space=pltpu.VMEM)
    hbm = pl.BlockSpec(memory_space=pltpu.HBM)
    slots = 2 * REACH + 1
    dma = pltpu.SemaphoreType.DMA
    block = pltpu.VMEM((4, 2, waves, gates), jnp.bfloat16)
    rows = [a.reshape(1, -1) for a in (
        fraction, gate_shift, aperture_start, aperture_end, doppler, chirp_rate)]
    return pl.pallas_call(
        functools.partial(kernel, n),
        out_shape=(jax.ShapeDtypeStruct((2, waves, gates), jnp.bfloat16),
                   jax.ShapeDtypeStruct((waves, gates), f32)),
        in_specs=[hbm] * 7,
        out_specs=(vmem, vmem),
        scratch_shapes=[pltpu.VMEM(pulses.shape, pulses.dtype)] + [pltpu.VMEM(a.shape, a.dtype) for a in rows] + [
            pltpu.VMEM((8, waves), f32),
            pltpu.VMEM((8, pulse_count), f32),
            pltpu.VMEM((pulse_count, 2 * gates), jnp.bfloat16),
            pltpu.VMEM((2 * waves, pulse_count), jnp.bfloat16),
            pltpu.VMEM((waves, 8), f32),
            pltpu.VMEM((pulse_count, 8), f32),
            pltpu.VMEM((slots, 8, waves), f32),
            block, block, block, block,
            pltpu.VMEM((2, waves, gates), f32),
            pltpu.VMEM((waves + 2 * LOOK, gates), f32),
            dma((7,)), dma((slots,)), dma((slots,)), dma((4,)), dma((4,)), dma((4,)), dma((4,)), dma((2,)), dma((2,)),
        ],
        compiler_params=pltpu.CompilerParams(
            collective_id=0, has_side_effects=True, vmem_limit_bytes=60 * 1024 * 1024),
    )(pulses, *rows)


def solution(mesh):
    seg = P(("arcs", "seg"))
    return jax.shard_map(
        shards,
        mesh=mesh,
        in_specs=(P(None, ("arcs", "seg"), None), seg, seg, seg, seg, seg, seg),
        out_specs=(P(None, ("arcs", "seg"), None), P(("arcs", "seg"), None)),
        check_vma=False,
    )
```

```python
import functools
import math

import jax
import jax.numpy as jnp
from jax import lax
from jax.experimental import pallas as pl
from jax.experimental.pallas import tpu as pltpu
from jax.sharding import PartitionSpec as P

REACH = 4
LOOK = 8
SHIFT_BITS = 4
ROWS = 32
MESH = pl.DeviceIdType.MESH

SIN = (3.141592640130708, -5.167710083507871, 2.550077523214076, -0.5982912856170641, 0.07765766029898877)
COS = (0.9999999532476084, -4.93479283061964, 4.058411352862407, -1.3318765680796267, 0.21968961109548557)


def horner(coefs, u):
    result = coefs[-1] * u + coefs[-2]
    for c in coefs[-3::-1]:
        result = result * u + c
    return result


def kernel(n, pulses_hbm, fraction_hbm, shift_hbm, start_hbm, end_hbm, doppler_hbm, chirp_hbm,
           focus_hbm, look_hbm, focus_ref, look_ref,
           pulses_ref, fraction_ref, shift_ref, start_ref, end_ref, doppler_ref, chirp_ref,
           params_ref, gates_ref, mig, wts, cols, gcols, pbuf, helpb, gotb, sendb, recvb, acc, power,
           outsem, insem, psend, precv, gsend, grecv, tsend, trecv, hsend, hrecv):
    me = lax.axis_index("seg")
    core = lax.rem(me, 2)
    way = 1 - 2 * core
    mate = me + way
    pulse_count, gates = pulses_ref.shape[1:]
    waves = params_ref.shape[1]
    scale = 1.0 / float(REACH * pulse_count)

    def exists(d):
        return (d >= 0) & (d < n)

    def loop(count, body):
        def step(i, carry):
            body(i)
            return carry
        lax.fori_loop(0, count, step, 0)

    def each(body):
        def peer(i):
            @pl.when((i != REACH) & exists(me + i - REACH))
            def _():
                body(i, me + i - REACH)
        loop(2 * REACH + 1, peer)

    barrier = pltpu.get_barrier_semaphore()

    def greet(i, peer):
        pl.semaphore_signal(barrier, inc=1, device_id={"seg": peer}, device_id_type=MESH)

    each(greet)
    loads = [pltpu.make_async_copy(src, dst, insem.at[i]) for i, (src, dst) in enumerate((
        (start_hbm, start_ref), (end_hbm, end_ref), (doppler_hbm, doppler_ref), (chirp_hbm, chirp_ref),
        (fraction_hbm, fraction_ref), (shift_hbm, shift_ref), (pulses_hbm, pulses_ref)))]
    for load in loads:
        load.start()
    for load in loads[:4]:
        load.wait()
    start, end = start_ref[...], end_ref[...]
    f32 = jnp.float32
    turn = 1.0 / (2.0 * math.pi)
    params_ref[0:1, :] = lax.shift_right_arithmetic(start + end, 1).astype(f32)
    params_ref[1:2, :] = start.astype(f32)
    params_ref[2:3, :] = end.astype(f32)
    params_ref[3:4, :] = chirp_ref[...] * turn
    params_ref[4:5, :] = doppler_ref[...] * turn
    params_ref[5:6, :] = lax.rsqrt((end - start).astype(f32))
    params_ref[6:8, :] = jnp.zeros((2, waves), f32)
    def params_copy(i, target):
        return pltpu.make_async_remote_copy(
            src_ref=params_ref, dst_ref=pbuf.at[i], send_sem=psend.at[i], recv_sem=precv.at[i],
            device_id={"seg": target}, device_id_type=MESH)

    for load in loads[4:]:
        load.wait()
    gates_ref[0:1, :] = fraction_ref[...]
    gates_ref[1:2, :] = shift_ref[...].astype(f32)
    gates_ref[2:8, :] = jnp.zeros((6, pulse_count), f32)
    gcols[...] = gates_ref[...].T
    lane = lax.broadcasted_iota(jnp.int32, (ROWS, gates), 1)

    def migrate_rows(q, carry):
        rows = pl.ds(pl.multiple_of(q * ROWS, ROWS), ROWS)
        frac = gcols[rows, 0:1]
        shift = gcols[rows, 1:2].astype(jnp.int32)
        for c in range(2):
            x = pulses_ref[c, rows, :].astype(jnp.float32)
            nxt = jnp.where(lane == gates - 1, 0.0, pltpu.roll(x, gates - 1, 1))
            z = (1.0 - frac) * x + frac * nxt
            for b in range(SHIFT_BITS):
                z = jnp.where((shift & (1 << b)) != 0, pltpu.roll(z, gates - (1 << b), 1), z)
            z = jnp.where(lane + shift < gates, z, 0.0)
            mig[rows, c * gates:(c + 1) * gates] = z.astype(jnp.bfloat16)
        return carry

    chunks = pulse_count // ROWS
    lax.fori_loop(0, chunks // 2, migrate_rows, 0, unroll=4)
    pl.semaphore_wait(barrier, jnp.minimum(me, REACH) + jnp.minimum(n - 1 - me, REACH))
    each(lambda i, peer: params_copy(2 * REACH - i, peer).start())
    lax.fori_loop(chunks // 2, chunks, migrate_rows, 0, unroll=4)

    pulse = (me * pulse_count + lax.broadcasted_iota(jnp.int32, (ROWS, pulse_count), 1)).astype(jnp.float32)

    def term(packed):
        cols[...] = packed.T

        def weigh(q, carry):
            rows = pl.ds(pl.multiple_of(q * ROWS, ROWS), ROWS)
            low = pl.ds(pl.multiple_of(waves + q * ROWS, ROWS), ROWS)
            center, start, end = cols[rows, 0:1], cols[rows, 1:2], cols[rows, 2:3]
            rate, slope, amp = cols[rows, 3:4], cols[rows, 4:5], cols[rows, 5:6]
            r = (pulse - center) * scale
            t = r * (rate * r + slope)
            t = t - jnp.floor(t + 0.5)
            u = t * t
            s = t * horner(SIN, u)
            c = horner(COS, u)
            a = jnp.where((pulse >= start) & (pulse < end), amp, 0.0)
            twice = (a + a) * s
            wts[rows, :] = (a - twice * s).astype(jnp.bfloat16)
            wts[low, :] = (twice * c).astype(jnp.bfloat16)
            return carry

        lax.fori_loop(0, waves // ROWS, weigh, 0, unroll=True)
        real = jnp.dot(wts[...], mig[:, :gates], preferred_element_type=jnp.float32)
        imag = jnp.dot(wts[...], mig[:, gates:], preferred_element_type=jnp.float32)
        return real[:waves] - imag[waves:], imag[:waves] + real[waves:]

    def term_for(o):
        i = o + REACH
        params_copy(i, me + o).wait_recv()
        return term(pbuf[i])

    def own(k):
        return 4 - 2 * k - 2 * (k // 2)

    def help_copy(k):
        return pltpu.make_async_remote_copy(
            src_ref=helpb.at[k], dst_ref=gotb.at[k], send_sem=gsend.at[k], recv_sem=grecv.at[k],
            device_id={"seg": mate}, device_id_type=MESH)

    def sum_copy(k, target):
        return pltpu.make_async_remote_copy(
            src_ref=sendb.at[k], dst_ref=recvb.at[k], send_sem=tsend.at[k], recv_sem=trecv.at[k],
            device_id={"seg": target}, device_id_type=MESH)

    def alone(k):
        @pl.when(exists(me + way * own(k)))
        def _():
            real, imag = term_for(way * own(k))
            sendb[k, 0] = real.astype(jnp.bfloat16)
            sendb[k, 1] = imag.astype(jnp.bfloat16)
            sum_copy(k, me + way * own(k)).start()

    def assist(k):
        o = way * (1 - own(k))

        @pl.when(exists(me + o))
        def _():
            real, imag = term_for(o)
            helpb[k, 0] = real.astype(jnp.bfloat16)
            helpb[k, 1] = imag.astype(jnp.bfloat16)
            help_copy(k).start()

    def shared(k):
        @pl.when(exists(me + way * own(k)))
        def _():
            real, imag = term_for(way * own(k))
            help_copy(k).wait_recv()
            sendb[k, 0] = (real + gotb[k, 0].astype(f32)).astype(jnp.bfloat16)
            sendb[k, 1] = (imag + gotb[k, 1].astype(f32)).astype(jnp.bfloat16)
            sum_copy(k, me + way * own(k)).start()

    acc[0], acc[1] = term(params_ref[...])
    alone(3)
    assist(0)
    assist(1)
    shared(0)
    assist(2)
    shared(1)
    shared(2)
    real, imag = term_for(way)
    helpb[3, 0] = real.astype(jnp.bfloat16)
    helpb[3, 1] = imag.astype(jnp.bfloat16)
    help_copy(3).start()
    help_copy(3).wait_recv()
    acc[0] += gotb[3, 0].astype(f32)
    acc[1] += gotb[3, 1].astype(f32)

    def take(j):
        k = 3 - j

        @pl.when(exists(me - way * own(k)))
        def _():
            sum_copy(k, me - way * own(k)).wait_recv()
            acc[0] += recvb[k, 0].astype(f32)
            acc[1] += recvb[k, 1].astype(f32)

    loop(4, take)
    power[LOOK:LOOK + waves, :] = acc[0] * acc[0] + acc[1] * acc[1]

    def halo_copy(side):
        low = LOOK if side == 0 else waves
        into = LOOK + waves if side == 0 else 0
        target = me - 1 if side == 0 else me + 1
        return pltpu.make_async_remote_copy(
            src_ref=power.at[pl.ds(low, LOOK)], dst_ref=power.at[pl.ds(into, LOOK)],
            send_sem=hsend.at[side], recv_sem=hrecv.at[side],
            device_id={"seg": target}, device_id_type=MESH)

    @pl.when(me > 0)
    def _():
        halo_copy(0).start()

    @pl.when(me < n - 1)
    def _():
        halo_copy(1).start()

    @pl.when(me == 0)
    def _():
        power[0:LOOK, :] = jnp.zeros((LOOK, gates), jnp.float32)

    @pl.when(me == n - 1)
    def _():
        power[LOOK + waves:, :] = jnp.zeros((LOOK, gates), jnp.float32)

    focus_ref[...] = acc[...].astype(jnp.bfloat16)
    focus_out = pltpu.make_async_copy(focus_ref, focus_hbm, outsem.at[0])
    look_out = pltpu.make_async_copy(look_ref, look_hbm, outsem.at[1])
    focus_out.start()

    def average(low, count):
        size = count + 2 * LOOK
        total = power[low:low + size, :]
        last = total[2 * LOOK:]
        step = 1
        while step < 2 * LOOK:
            size -= step
            total = total[:size] + total[step:step + size]
            step *= 2
        look_ref[low:low + count, :] = (total[:count] + last) * (1.0 / float(2 * LOOK + 1))

    average(LOOK, waves - 2 * LOOK)
    each(lambda i, peer: params_copy(2 * REACH - i, peer).wait_send())

    def drain(k):
        @pl.when(exists(me + way * own(k)))
        def _():
            sum_copy(k, me + way * own(k)).wait_send()

    loop(4, drain)

    def drain_help(k):
        @pl.when(exists(me + way * (1 - own(k))))
        def _():
            help_copy(k).wait_send()

    loop(3, drain_help)
    help_copy(3).wait_send()

    @pl.when(me > 0)
    def _():
        halo_copy(0).wait_send()
        halo_copy(1).wait_recv()

    @pl.when(me < n - 1)
    def _():
        halo_copy(1).wait_send()
        halo_copy(0).wait_recv()

    average(0, LOOK)
    average(waves - LOOK, LOOK)
    look_out.start()
    focus_out.wait()
    look_out.wait()


def hand_over(focus_in, look_in, focus_out, look_out, sems):
    copies = [pltpu.make_async_copy(focus_in, focus_out, sems.at[0]),
              pltpu.make_async_copy(look_in, look_out, sems.at[1])]
    for copy in copies:
        copy.start()
    for copy in copies:
        copy.wait()


def shards(pulses, fraction, gate_shift, aperture_start, aperture_end, doppler, chirp_rate):
    n = lax.axis_size("seg")
    pulse_count, gates = pulses.shape[1:]
    waves = aperture_start.shape[0]
    f32 = jnp.float32
    hbm = pl.BlockSpec(memory_space=pltpu.HBM)
    slots = 2 * REACH + 1
    dma = pltpu.SemaphoreType.DMA
    block = pltpu.VMEM((4, 2, waves, gates), jnp.bfloat16)
    rows = [a.reshape(1, -1) for a in (
        fraction, gate_shift, aperture_start, aperture_end, doppler, chirp_rate)]
    outs = (jax.ShapeDtypeStruct((2, waves, gates), jnp.bfloat16), jax.ShapeDtypeStruct((waves, gates), f32))
    results = pl.pallas_call(
        functools.partial(kernel, n),
        out_shape=outs,
        in_specs=[hbm] * 7,
        out_specs=(hbm, hbm),
        scratch_shapes=[pltpu.VMEM(o.shape, o.dtype) for o in outs] + [pltpu.VMEM(pulses.shape, pulses.dtype)] + [pltpu.VMEM(a.shape, a.dtype) for a in rows] + [
            pltpu.VMEM((8, waves), f32),
            pltpu.VMEM((8, pulse_count), f32),
            pltpu.VMEM((pulse_count, 2 * gates), jnp.bfloat16),
            pltpu.VMEM((2 * waves, pulse_count), jnp.bfloat16),
            pltpu.VMEM((waves, 8), f32),
            pltpu.VMEM((pulse_count, 8), f32),
            pltpu.VMEM((slots, 8, waves), f32),
            block, block, block, block,
            pltpu.VMEM((2, waves, gates), f32),
            pltpu.VMEM((waves + 2 * LOOK, gates), f32),
            dma((2,)), dma((7,)), dma((slots,)), dma((slots,)), dma((4,)), dma((4,)), dma((4,)), dma((4,)), dma((2,)), dma((2,)),
        ],
        compiler_params=pltpu.CompilerParams(
            collective_id=0, has_side_effects=True, vmem_limit_bytes=60 * 1024 * 1024),
    )(pulses, *rows)
    return pl.pallas_call(
        hand_over, out_shape=outs, in_specs=[hbm, hbm], out_specs=(hbm, hbm), scratch_shapes=[dma((2,))],
    )(*results)


def solution(mesh):
    seg = P(("arcs", "seg"))
    return jax.shard_map(
        shards,
        mesh=mesh,
        in_specs=(P(None, ("arcs", "seg"), None), seg, seg, seg, seg, seg, seg),
        out_specs=(P(None, ("arcs", "seg"), None), P(("arcs", "seg"), None)),
        check_vma=False,
    )
```

```python
import functools
import math

import jax
import jax.numpy as jnp
from jax import lax
from jax.experimental import pallas as pl
from jax.experimental.pallas import tpu as pltpu
from jax.sharding import PartitionSpec as P

REACH = 4
LOOK = 8
SHIFT_BITS = 4
ROWS = 32
MESH = pl.DeviceIdType.MESH

SIN = (3.141592640130708, -5.167710083507871, 2.550077523214076, -0.5982912856170641, 0.07765766029898877)
COS = (0.9999999532476084, -4.93479283061964, 4.058411352862407, -1.3318765680796267, 0.21968961109548557)


def horner(coefs, u):
    result = coefs[-1] * u + coefs[-2]
    for c in coefs[-3::-1]:
        result = result * u + c
    return result


def kernel(n, pulses_hbm, fraction_hbm, shift_hbm, start_hbm, end_hbm, doppler_hbm, chirp_hbm,
           focus_ref, look_ref,
           pulses_ref, fraction_ref, shift_ref, start_ref, end_ref, doppler_ref, chirp_ref,
           params_ref, gates_ref, mig, wts, cols, gcols, pbuf, helpb, gotb, sendb, recvb, acc, power,
           insem, psend, precv, gsend, grecv, tsend, trecv, hsend, hrecv):
    me = lax.axis_index("seg")
    core = lax.rem(me, 2)
    way = 1 - 2 * core
    mate = me + way
    pulse_count, gates = pulses_ref.shape[1:]
    waves = params_ref.shape[1]
    scale = 1.0 / float(REACH * pulse_count)

    def exists(d):
        return (d >= 0) & (d < n)

    def loop(count, body):
        def step(i, carry):
            body(i)
            return carry
        lax.fori_loop(0, count, step, 0)

    def each(body):
        def peer(i):
            @pl.when((i != REACH) & exists(me + i - REACH))
            def _():
                body(i, me + i - REACH)
        loop(2 * REACH + 1, peer)

    barrier = pltpu.get_barrier_semaphore()

    def greet(i, peer):
        pl.semaphore_signal(barrier, inc=1, device_id={"seg": peer}, device_id_type=MESH)

    each(greet)
    loads = [pltpu.make_async_copy(src, dst, insem.at[i]) for i, (src, dst) in enumerate((
        (start_hbm, start_ref), (end_hbm, end_ref), (doppler_hbm, doppler_ref), (chirp_hbm, chirp_ref),
        (fraction_hbm, fraction_ref), (shift_hbm, shift_ref), (pulses_hbm, pulses_ref)))]
    for load in loads:
        load.start()
    for load in loads[:4]:
        load.wait()
    start, end = start_ref[...], end_ref[...]
    f32 = jnp.float32
    turn = 1.0 / (2.0 * math.pi)
    params_ref[0:1, :] = lax.shift_right_arithmetic(start + end, 1).astype(f32)
    params_ref[1:2, :] = start.astype(f32)
    params_ref[2:3, :] = end.astype(f32)
    params_ref[3:4, :] = chirp_ref[...] * turn
    params_ref[4:5, :] = doppler_ref[...] * turn
    params_ref[5:6, :] = lax.rsqrt((end - start).astype(f32))
    params_ref[6:8, :] = jnp.zeros((2, waves), f32)
    pl.semaphore_wait(barrier, jnp.minimum(me, REACH) + jnp.minimum(n - 1 - me, REACH))

    def params_copy(i, target):
        return pltpu.make_async_remote_copy(
            src_ref=params_ref, dst_ref=pbuf.at[i], send_sem=psend.at[i], recv_sem=precv.at[i],
            device_id={"seg": target}, device_id_type=MESH)

    each(lambda i, peer: params_copy(2 * REACH - i, peer).start())
    for load in loads[4:]:
        load.wait()
    gates_ref[0:1, :] = fraction_ref[...]
    gates_ref[1:2, :] = shift_ref[...].astype(f32)
    gates_ref[2:8, :] = jnp.zeros((6, pulse_count), f32)
    gcols[...] = gates_ref[...].T
    lane = lax.broadcasted_iota(jnp.int32, (ROWS, gates), 1)

    def migrate_rows(q, carry):
        rows = pl.ds(pl.multiple_of(q * ROWS, ROWS), ROWS)
        frac = gcols[rows, 0:1]
        shift = gcols[rows, 1:2].astype(jnp.int32)
        for c in range(2):
            x = pulses_ref[c, rows, :].astype(jnp.float32)
            nxt = jnp.where(lane == gates - 1, 0.0, pltpu.roll(x, gates - 1, 1))
            z = (1.0 - frac) * x + frac * nxt
            for b in range(SHIFT_BITS):
                z = jnp.where((shift & (1 << b)) != 0, pltpu.roll(z, gates - (1 << b), 1), z)
            z = jnp.where(lane + shift < gates, z, 0.0)
            mig[rows, c * gates:(c + 1) * gates] = z.astype(jnp.bfloat16)
        return carry

    lax.fori_loop(0, pulse_count // ROWS, migrate_rows, 0, unroll=4)

    pulse = (me * pulse_count + lax.broadcasted_iota(jnp.int32, (ROWS, pulse_count), 1)).astype(jnp.float32)

    def term(packed):
        cols[...] = packed.T

        def weigh(q, carry):
            rows = pl.ds(pl.multiple_of(q * ROWS, ROWS), ROWS)
            low = pl.ds(pl.multiple_of(waves + q * ROWS, ROWS), ROWS)
            center, start, end = cols[rows, 0:1], cols[rows, 1:2], cols[rows, 2:3]
            rate, slope, amp = cols[rows, 3:4], cols[rows, 4:5], cols[rows, 5:6]
            r = (pulse - center) * scale
            t = r * (rate * r + slope)
            t = t - jnp.floor(t + 0.5)
            u = t * t
            s = t * horner(SIN, u)
            c = horner(COS, u)
            a = jnp.where((pulse >= start) & (pulse < end), amp, 0.0)
            twice = (a + a) * s
            wts[rows, :] = (a - twice * s).astype(jnp.bfloat16)
            wts[low, :] = (twice * c).astype(jnp.bfloat16)
            return carry

        lax.fori_loop(0, waves // ROWS, weigh, 0, unroll=True)
        real = jnp.dot(wts[...], mig[:, :gates], preferred_element_type=jnp.float32)
        imag = jnp.dot(wts[...], mig[:, gates:], preferred_element_type=jnp.float32)
        return real[:waves] - imag[waves:], imag[:waves] + real[waves:]

    def term_for(o):
        i = o + REACH
        params_copy(i, me + o).wait_recv()
        return term(pbuf[i])

    def own(k):
        return 4 - 2 * k - 2 * lax.div(k, 2)

    def help_copy(k):
        return pltpu.make_async_remote_copy(
            src_ref=helpb.at[k], dst_ref=gotb.at[k], send_sem=gsend.at[k], recv_sem=grecv.at[k],
            device_id={"seg": mate}, device_id_type=MESH)

    def sum_copy(k, target):
        return pltpu.make_async_remote_copy(
            src_ref=sendb.at[k], dst_ref=recvb.at[k], send_sem=tsend.at[k], recv_sem=trecv.at[k],
            device_id={"seg": target}, device_id_type=MESH)

    def alone(k):
        @pl.when(exists(me + way * own(k)))
        def _():
            real, imag = term_for(way * own(k))
            sendb[k, 0] = real.astype(jnp.bfloat16)
            sendb[k, 1] = imag.astype(jnp.bfloat16)
            sum_copy(k, me + way * own(k)).start()

    def assist(k):
        o = way * (1 - own(k))

        @pl.when(exists(me + o))
        def _():
            real, imag = term_for(o)
            helpb[k, 0] = real.astype(jnp.bfloat16)
            helpb[k, 1] = imag.astype(jnp.bfloat16)
            help_copy(k).start()

    def shared(k):
        @pl.when(exists(me + way * own(k)))
        def _():
            real, imag = term_for(way * own(k))
            help_copy(k).wait_recv()
            sendb[k, 0] = (real + gotb[k, 0].astype(f32)).astype(jnp.bfloat16)
            sendb[k, 1] = (imag + gotb[k, 1].astype(f32)).astype(jnp.bfloat16)
            sum_copy(k, me + way * own(k)).start()

    loop(1, lambda k: alone(k + 3))
    loop(3, assist)
    loop(3, shared)
    real, imag = term_for(way)
    helpb[3, 0] = real.astype(jnp.bfloat16)
    helpb[3, 1] = imag.astype(jnp.bfloat16)
    help_copy(3).start()
    real, imag = term(params_ref[...])
    help_copy(3).wait_recv()
    acc[0] = real + gotb[3, 0].astype(f32)
    acc[1] = imag + gotb[3, 1].astype(f32)

    def take(j):
        k = 3 - j

        @pl.when(exists(me - way * own(k)))
        def _():
            sum_copy(k, me - way * own(k)).wait_recv()
            acc[0] += recvb[k, 0].astype(f32)
            acc[1] += recvb[k, 1].astype(f32)

    loop(4, take)
    power[LOOK:LOOK + waves, :] = acc[0] * acc[0] + acc[1] * acc[1]

    def halo_copy(side):
        low = LOOK if side == 0 else waves
        into = LOOK + waves if side == 0 else 0
        target = me - 1 if side == 0 else me + 1
        return pltpu.make_async_remote_copy(
            src_ref=power.at[pl.ds(low, LOOK)], dst_ref=power.at[pl.ds(into, LOOK)],
            send_sem=hsend.at[side], recv_sem=hrecv.at[side],
            device_id={"seg": target}, device_id_type=MESH)

    @pl.when(me > 0)
    def _():
        halo_copy(0).start()

    @pl.when(me < n - 1)
    def _():
        halo_copy(1).start()

    @pl.when(me == 0)
    def _():
        power[0:LOOK, :] = jnp.zeros((LOOK, gates), jnp.float32)

    @pl.when(me == n - 1)
    def _():
        power[LOOK + waves:, :] = jnp.zeros((LOOK, gates), jnp.float32)

    focus_ref[...] = acc[...].astype(jnp.bfloat16)

    def average(low, count):
        size = count + 2 * LOOK
        total = power[low:low + size, :]
        last = total[2 * LOOK:]
        step = 1
        while step < 2 * LOOK:
            size -= step
            total = total[:size] + total[step:step + size]
            step *= 2
        look_ref[low:low + count, :] = (total[:count] + last) * (1.0 / float(2 * LOOK + 1))

    average(LOOK, waves - 2 * LOOK)
    each(lambda i, peer: params_copy(2 * REACH - i, peer).wait_send())

    def drain(k):
        @pl.when(exists(me + way * own(k)))
        def _():
            sum_copy(k, me + way * own(k)).wait_send()

    loop(4, drain)

    def drain_help(k):
        @pl.when(exists(me + way * (1 - own(k))))
        def _():
            help_copy(k).wait_send()

    loop(3, drain_help)
    help_copy(3).wait_send()

    @pl.when(me > 0)
    def _():
        halo_copy(0).wait_send()
        halo_copy(1).wait_recv()

    @pl.when(me < n - 1)
    def _():
        halo_copy(1).wait_send()
        halo_copy(0).wait_recv()

    average(0, LOOK)
    average(waves - LOOK, LOOK)


def hand_over(focus_in, look_in, focus_out, look_out, focus, look, sems):
    arrays = ((focus_in, focus, focus_out), (look_in, look, look_out))
    loads = [pltpu.make_async_copy(a, b, sems.at[i]) for i, (a, b, _) in enumerate(arrays)]
    stores = [pltpu.make_async_copy(b, c, sems.at[2 + i]) for i, (_, b, c) in enumerate(arrays)]
    for load in loads:
        load.start()
    for load, store in zip(loads, stores):
        load.wait()
        store.start()
    for store in stores:
        store.wait()


def shards(pulses, fraction, gate_shift, aperture_start, aperture_end, doppler, chirp_rate):
    n = lax.axis_size("seg")
    pulse_count, gates = pulses.shape[1:]
    waves = aperture_start.shape[0]
    f32 = jnp.float32
    vmem = pl.BlockSpec(memory_space=pltpu.VMEM)
    hbm = pl.BlockSpec(memory_space=pltpu.HBM)
    slots = 2 * REACH + 1
    dma = pltpu.SemaphoreType.DMA
    block = pltpu.VMEM((4, 2, waves, gates), jnp.bfloat16)
    rows = [a.reshape(1, -1) for a in (
        fraction, gate_shift, aperture_start, aperture_end, doppler, chirp_rate)]
    outs = (jax.ShapeDtypeStruct((2, waves, gates), jnp.bfloat16), jax.ShapeDtypeStruct((waves, gates), f32))
    results = pl.pallas_call(
        functools.partial(kernel, n),
        out_shape=outs,
        in_specs=[hbm] * 7,
        out_specs=(vmem, vmem),
        scratch_shapes=[pltpu.VMEM(pulses.shape, pulses.dtype)] + [pltpu.VMEM(a.shape, a.dtype) for a in rows] + [
            pltpu.VMEM((8, waves), f32),
            pltpu.VMEM((8, pulse_count), f32),
            pltpu.VMEM((pulse_count, 2 * gates), jnp.bfloat16),
            pltpu.VMEM((2 * waves, pulse_count), jnp.bfloat16),
            pltpu.VMEM((waves, 8), f32),
            pltpu.VMEM((pulse_count, 8), f32),
            pltpu.VMEM((slots, 8, waves), f32),
            block, block, block, block,
            pltpu.VMEM((2, waves, gates), f32),
            pltpu.VMEM((waves + 2 * LOOK, gates), f32),
            dma((7,)), dma((slots,)), dma((slots,)), dma((4,)), dma((4,)), dma((4,)), dma((4,)), dma((2,)), dma((2,)),
        ],
        compiler_params=pltpu.CompilerParams(
            collective_id=0, has_side_effects=True, vmem_limit_bytes=60 * 1024 * 1024),
    )(pulses, *rows)
    return pl.pallas_call(
        hand_over, out_shape=outs, in_specs=[hbm, hbm], out_specs=(hbm, hbm),
        scratch_shapes=[pltpu.VMEM(o.shape, o.dtype) for o in outs] + [dma((4,))],
        compiler_params=pltpu.CompilerParams(vmem_limit_bytes=60 * 1024 * 1024),
    )(*results)


def solution(mesh):
    seg = P(("arcs", "seg"))
    return jax.shard_map(
        shards,
        mesh=mesh,
        in_specs=(P(None, ("arcs", "seg"), None), seg, seg, seg, seg, seg, seg),
        out_specs=(P(None, ("arcs", "seg"), None), P(("arcs", "seg"), None)),
        check_vma=False,
    )
```

```python
import functools
import math

import jax
import jax.numpy as jnp
from jax import lax
from jax.experimental import pallas as pl
from jax.experimental.pallas import tpu as pltpu
from jax.sharding import PartitionSpec as P

REACH = 4
LOOK = 8
SHIFT_BITS = 4
ROWS = 32
MESH = pl.DeviceIdType.MESH

SIN = (3.141592640130708, -5.167710083507871, 2.550077523214076, -0.5982912856170641, 0.07765766029898877)
COS = (0.9999999532476084, -4.93479283061964, 4.058411352862407, -1.3318765680796267, 0.21968961109548557)


def horner(coefs, u):
    result = coefs[-1] * u + coefs[-2]
    for c in coefs[-3::-1]:
        result = result * u + c
    return result


def kernel(n, pulses_hbm, fraction_hbm, shift_hbm, start_hbm, end_hbm, doppler_hbm, chirp_hbm,
           focus_ref, look_ref,
           pulses_ref, fraction_ref, shift_ref, start_ref, end_ref, doppler_ref, chirp_ref,
           params_ref, gates_ref, mig, wts, cols, gcols, pbuf, helpb, gotb, sendb, recvb, acc, power,
           insem, psend, precv, gsend, grecv, tsend, trecv, hsend, hrecv):
    me = lax.axis_index("seg")
    core = lax.rem(me, 2)
    way = 1 - 2 * core
    mate = me + way
    pulse_count, gates = pulses_ref.shape[1:]
    waves = params_ref.shape[1]
    scale = 1.0 / float(REACH * pulse_count)

    def exists(d):
        return (d >= 0) & (d < n)

    def loop(count, body):
        def step(i, carry):
            body(i)
            return carry
        lax.fori_loop(0, count, step, 0)

    def each(body):
        def peer(i):
            @pl.when((i != REACH) & exists(me + i - REACH))
            def _():
                body(i, me + i - REACH)
        loop(2 * REACH + 1, peer)

    barrier = pltpu.get_barrier_semaphore()

    def greet(i, peer):
        pl.semaphore_signal(barrier, inc=1, device_id={"seg": peer}, device_id_type=MESH)

    each(greet)
    loads = [pltpu.make_async_copy(src, dst, insem.at[i]) for i, (src, dst) in enumerate((
        (start_hbm, start_ref), (end_hbm, end_ref), (doppler_hbm, doppler_ref), (chirp_hbm, chirp_ref),
        (fraction_hbm, fraction_ref), (shift_hbm, shift_ref), (pulses_hbm, pulses_ref)))]
    for load in loads:
        load.start()
    for load in loads[:4]:
        load.wait()
    start, end = start_ref[...], end_ref[...]
    f32 = jnp.float32
    turn = 1.0 / (2.0 * math.pi)
    params_ref[0:1, :] = lax.shift_right_arithmetic(start + end, 1).astype(f32)
    params_ref[1:2, :] = start.astype(f32)
    params_ref[2:3, :] = end.astype(f32)
    params_ref[3:4, :] = chirp_ref[...] * turn
    params_ref[4:5, :] = doppler_ref[...] * turn
    params_ref[5:6, :] = lax.rsqrt((end - start).astype(f32))
    params_ref[6:8, :] = jnp.zeros((2, waves), f32)
    pl.semaphore_wait(barrier, jnp.minimum(me, REACH) + jnp.minimum(n - 1 - me, REACH))

    def params_copy(i, target):
        return pltpu.make_async_remote_copy(
            src_ref=params_ref, dst_ref=pbuf.at[i], send_sem=psend.at[i], recv_sem=precv.at[i],
            device_id={"seg": target}, device_id_type=MESH)

    each(lambda i, peer: params_copy(2 * REACH - i, peer).start())
    for load in loads[4:]:
        load.wait()
    gates_ref[0:1, :] = fraction_ref[...]
    gates_ref[1:2, :] = shift_ref[...].astype(f32)
    gates_ref[2:8, :] = jnp.zeros((6, pulse_count), f32)
    gcols[...] = gates_ref[...].T
    lane = lax.broadcasted_iota(jnp.int32, (ROWS, gates), 1)

    def migrate_rows(q, carry):
        rows = pl.ds(pl.multiple_of(q * ROWS, ROWS), ROWS)
        frac = gcols[rows, 0:1]
        shift = gcols[rows, 1:2].astype(jnp.int32)
        for c in range(2):
            x = pulses_ref[c, rows, :].astype(jnp.float32)
            nxt = jnp.where(lane == gates - 1, 0.0, pltpu.roll(x, gates - 1, 1))
            z = (1.0 - frac) * x + frac * nxt
            for b in range(SHIFT_BITS):
                z = jnp.where((shift & (1 << b)) != 0, pltpu.roll(z, gates - (1 << b), 1), z)
            z = jnp.where(lane + shift < gates, z, 0.0)
            mig[rows, c * gates:(c + 1) * gates] = z.astype(jnp.bfloat16)
        return carry

    lax.fori_loop(0, pulse_count // ROWS, migrate_rows, 0, unroll=4)

    pulse = (me * pulse_count + lax.broadcasted_iota(jnp.int32, (ROWS, pulse_count), 1)).astype(jnp.float32)

    def term(packed):
        cols[...] = packed.T

        def weigh(q, carry):
            rows = pl.ds(pl.multiple_of(q * ROWS, ROWS), ROWS)
            low = pl.ds(pl.multiple_of(waves + q * ROWS, ROWS), ROWS)
            center, start, end = cols[rows, 0:1], cols[rows, 1:2], cols[rows, 2:3]
            rate, slope, amp = cols[rows, 3:4], cols[rows, 4:5], cols[rows, 5:6]
            r = (pulse - center) * scale
            t = r * (rate * r + slope)
            t = t - jnp.floor(t + 0.5)
            u = t * t
            s = t * horner(SIN, u)
            c = horner(COS, u)
            a = jnp.where((pulse >= start) & (pulse < end), amp, 0.0)
            twice = (a + a) * s
            wts[rows, :] = (a - twice * s).astype(jnp.bfloat16)
            wts[low, :] = (twice * c).astype(jnp.bfloat16)
            return carry

        lax.fori_loop(0, waves // ROWS, weigh, 0, unroll=True)
        real = jnp.dot(wts[...], mig[:, :gates], preferred_element_type=jnp.float32)
        imag = jnp.dot(wts[...], mig[:, gates:], preferred_element_type=jnp.float32)
        return real[:waves] - imag[waves:], imag[:waves] + real[waves:]

    def term_for(o):
        i = o + REACH
        params_copy(i, me + o).wait_recv()
        return term(pbuf[i])

    def own(k):
        return 4 - 2 * k - 2 * lax.div(k, 2)

    def help_copy(k):
        return pltpu.make_async_remote_copy(
            src_ref=helpb.at[k], dst_ref=gotb.at[k], send_sem=gsend.at[k], recv_sem=grecv.at[k],
            device_id={"seg": mate}, device_id_type=MESH)

    def sum_copy(k, target):
        return pltpu.make_async_remote_copy(
            src_ref=sendb.at[k], dst_ref=recvb.at[k], send_sem=tsend.at[k], recv_sem=trecv.at[k],
            device_id={"seg": target}, device_id_type=MESH)

    def alone(k):
        @pl.when(exists(me + way * own(k)))
        def _():
            real, imag = term_for(way * own(k))
            sendb[k, 0] = real.astype(jnp.bfloat16)
            sendb[k, 1] = imag.astype(jnp.bfloat16)
            sum_copy(k, me + way * own(k)).start()

    def assist(k):
        o = way * (1 - own(k))

        @pl.when(exists(me + o))
        def _():
            real, imag = term_for(o)
            helpb[k, 0] = real.astype(jnp.bfloat16)
            helpb[k, 1] = imag.astype(jnp.bfloat16)
            help_copy(k).start()

    def shared(k):
        @pl.when(exists(me + way * own(k)))
        def _():
            real, imag = term_for(way * own(k))
            help_copy(k).wait_recv()
            sendb[k, 0] = (real + gotb[k, 0].astype(f32)).astype(jnp.bfloat16)
            sendb[k, 1] = (imag + gotb[k, 1].astype(f32)).astype(jnp.bfloat16)
            sum_copy(k, me + way * own(k)).start()

    loop(1, lambda k: alone(k + 3))
    loop(2, assist)
    loop(1, shared)
    loop(1, lambda k: assist(k + 2))
    loop(2, lambda k: shared(k + 1))
    real, imag = term_for(way)
    helpb[3, 0] = real.astype(jnp.bfloat16)
    helpb[3, 1] = imag.astype(jnp.bfloat16)
    help_copy(3).start()
    real, imag = term(params_ref[...])
    help_copy(3).wait_recv()
    acc[0] = real + gotb[3, 0].astype(f32)
    acc[1] = imag + gotb[3, 1].astype(f32)

    def take(j):
        k = 3 - j

        @pl.when(exists(me - way * own(k)))
        def _():
            sum_copy(k, me - way * own(k)).wait_recv()
            acc[0] += recvb[k, 0].astype(f32)
            acc[1] += recvb[k, 1].astype(f32)

    loop(4, take)
    power[LOOK:LOOK + waves, :] = acc[0] * acc[0] + acc[1] * acc[1]

    def halo_copy(side):
        low = LOOK if side == 0 else waves
        into = LOOK + waves if side == 0 else 0
        target = me - 1 if side == 0 else me + 1
        return pltpu.make_async_remote_copy(
            src_ref=power.at[pl.ds(low, LOOK)], dst_ref=power.at[pl.ds(into, LOOK)],
            send_sem=hsend.at[side], recv_sem=hrecv.at[side],
            device_id={"seg": target}, device_id_type=MESH)

    @pl.when(me > 0)
    def _():
        halo_copy(0).start()

    @pl.when(me < n - 1)
    def _():
        halo_copy(1).start()

    @pl.when(me == 0)
    def _():
        power[0:LOOK, :] = jnp.zeros((LOOK, gates), jnp.float32)

    @pl.when(me == n - 1)
    def _():
        power[LOOK + waves:, :] = jnp.zeros((LOOK, gates), jnp.float32)

    focus_ref[...] = acc[...].astype(jnp.bfloat16)

    def average(low, count):
        size = count + 2 * LOOK
        total = power[low:low + size, :]
        last = total[2 * LOOK:]
        step = 1
        while step < 2 * LOOK:
            size -= step
            total = total[:size] + total[step:step + size]
            step *= 2
        look_ref[low:low + count, :] = (total[:count] + last) * (1.0 / float(2 * LOOK + 1))

    average(LOOK, waves - 2 * LOOK)
    each(lambda i, peer: params_copy(2 * REACH - i, peer).wait_send())

    def drain(k):
        @pl.when(exists(me + way * own(k)))
        def _():
            sum_copy(k, me + way * own(k)).wait_send()

    loop(4, drain)

    def drain_help(k):
        @pl.when(exists(me + way * (1 - own(k))))
        def _():
            help_copy(k).wait_send()

    loop(3, drain_help)
    help_copy(3).wait_send()

    @pl.when(me > 0)
    def _():
        halo_copy(0).wait_send()
        halo_copy(1).wait_recv()

    @pl.when(me < n - 1)
    def _():
        halo_copy(1).wait_send()
        halo_copy(0).wait_recv()

    average(0, LOOK)
    average(waves - LOOK, LOOK)


def hand_over(focus_in, look_in, focus_out, look_out, focus, look, sems):
    arrays = ((focus_in, focus, focus_out), (look_in, look, look_out))
    loads = [pltpu.make_async_copy(a, b, sems.at[i]) for i, (a, b, _) in enumerate(arrays)]
    stores = [pltpu.make_async_copy(b, c, sems.at[2 + i]) for i, (_, b, c) in enumerate(arrays)]
    for load in loads:
        load.start()
    for load, store in zip(loads, stores):
        load.wait()
        store.start()
    for store in stores:
        store.wait()


def shards(pulses, fraction, gate_shift, aperture_start, aperture_end, doppler, chirp_rate):
    n = lax.axis_size("seg")
    pulse_count, gates = pulses.shape[1:]
    waves = aperture_start.shape[0]
    f32 = jnp.float32
    vmem = pl.BlockSpec(memory_space=pltpu.VMEM)
    hbm = pl.BlockSpec(memory_space=pltpu.HBM)
    slots = 2 * REACH + 1
    dma = pltpu.SemaphoreType.DMA
    block = pltpu.VMEM((4, 2, waves, gates), jnp.bfloat16)
    rows = [a.reshape(1, -1) for a in (
        fraction, gate_shift, aperture_start, aperture_end, doppler, chirp_rate)]
    outs = (jax.ShapeDtypeStruct((2, waves, gates), jnp.bfloat16), jax.ShapeDtypeStruct((waves, gates), f32))
    results = pl.pallas_call(
        functools.partial(kernel, n),
        out_shape=outs,
        in_specs=[hbm] * 7,
        out_specs=(vmem, vmem),
        scratch_shapes=[pltpu.VMEM(pulses.shape, pulses.dtype)] + [pltpu.VMEM(a.shape, a.dtype) for a in rows] + [
            pltpu.VMEM((8, waves), f32),
            pltpu.VMEM((8, pulse_count), f32),
            pltpu.VMEM((pulse_count, 2 * gates), jnp.bfloat16),
            pltpu.VMEM((2 * waves, pulse_count), jnp.bfloat16),
            pltpu.VMEM((waves, 8), f32),
            pltpu.VMEM((pulse_count, 8), f32),
            pltpu.VMEM((slots, 8, waves), f32),
            block, block, block, block,
            pltpu.VMEM((2, waves, gates), f32),
            pltpu.VMEM((waves + 2 * LOOK, gates), f32),
            dma((7,)), dma((slots,)), dma((slots,)), dma((4,)), dma((4,)), dma((4,)), dma((4,)), dma((2,)), dma((2,)),
        ],
        compiler_params=pltpu.CompilerParams(
            collective_id=0, has_side_effects=True, vmem_limit_bytes=60 * 1024 * 1024),
    )(pulses, *rows)
    return pl.pallas_call(
        hand_over, out_shape=outs, in_specs=[hbm, hbm], out_specs=(hbm, hbm),
        scratch_shapes=[pltpu.VMEM(o.shape, o.dtype) for o in outs] + [dma((4,))],
        compiler_params=pltpu.CompilerParams(vmem_limit_bytes=60 * 1024 * 1024),
    )(*results)


def solution(mesh):
    seg = P(("arcs", "seg"))
    return jax.shard_map(
        shards,
        mesh=mesh,
        in_specs=(P(None, ("arcs", "seg"), None), seg, seg, seg, seg, seg, seg),
        out_specs=(P(None, ("arcs", "seg"), None), P(("arcs", "seg"), None)),
        check_vma=False,
    )
```

```python
import functools
import math

import jax
import jax.numpy as jnp
from jax import lax
from jax.experimental import pallas as pl
from jax.experimental.pallas import tpu as pltpu
from jax.sharding import PartitionSpec as P

REACH = 4
LOOK = 8
SHIFT_BITS = 4
ROWS = 32
MESH = pl.DeviceIdType.MESH

SIN = (3.141592640130708, -5.167710083507871, 2.550077523214076, -0.5982912856170641, 0.07765766029898877)
COS = (0.9999999532476084, -4.93479283061964, 4.058411352862407, -1.3318765680796267, 0.21968961109548557)


def horner(coefs, u):
    result = coefs[-1] * u + coefs[-2]
    for c in coefs[-3::-1]:
        result = result * u + c
    return result


def kernel(n, pulses_hbm, fraction_hbm, shift_hbm, start_hbm, end_hbm, doppler_hbm, chirp_hbm,
           focus_ref, look_ref,
           pulses_ref, fraction_ref, shift_ref, start_ref, end_ref, doppler_ref, chirp_ref,
           params_ref, gates_ref, mig, wts, cols, gcols, pbuf, helpb, gotb, sendb, recvb, acc, power,
           insem, psend, precv, gsend, grecv, tsend, trecv, hsend, hrecv):
    me = lax.axis_index("seg")
    core = lax.rem(me, 2)
    way = 1 - 2 * core
    mate = me + way
    pulse_count, gates = pulses_ref.shape[1:]
    waves = params_ref.shape[1]
    scale = 1.0 / float(REACH * pulse_count)

    def exists(d):
        return (d >= 0) & (d < n)

    def loop(count, body):
        def step(i, carry):
            body(i)
            return carry
        lax.fori_loop(0, count, step, 0)

    def each(body):
        def peer(i):
            @pl.when((i != REACH) & exists(me + i - REACH))
            def _():
                body(i, me + i - REACH)
        loop(2 * REACH + 1, peer)

    barrier = pltpu.get_barrier_semaphore()

    def greet(i, peer):
        pl.semaphore_signal(barrier, inc=1, device_id={"seg": peer}, device_id_type=MESH)

    each(greet)
    loads = [pltpu.make_async_copy(src, dst, insem.at[i]) for i, (src, dst) in enumerate((
        (start_hbm, start_ref), (end_hbm, end_ref), (doppler_hbm, doppler_ref), (chirp_hbm, chirp_ref),
        (fraction_hbm, fraction_ref), (shift_hbm, shift_ref), (pulses_hbm, pulses_ref)))]
    for load in loads:
        load.start()
    for load in loads[:4]:
        load.wait()
    start, end = start_ref[...], end_ref[...]
    f32 = jnp.float32
    turn = 1.0 / (2.0 * math.pi)
    params_ref[0:1, :] = lax.shift_right_arithmetic(start + end, 1).astype(f32)
    params_ref[1:2, :] = start.astype(f32)
    params_ref[2:3, :] = end.astype(f32)
    params_ref[3:4, :] = chirp_ref[...] * turn
    params_ref[4:5, :] = doppler_ref[...] * turn
    params_ref[5:6, :] = lax.rsqrt((end - start).astype(f32))
    params_ref[6:8, :] = jnp.zeros((2, waves), f32)
    def params_copy(i, target):
        return pltpu.make_async_remote_copy(
            src_ref=params_ref, dst_ref=pbuf.at[i], send_sem=psend.at[i], recv_sem=precv.at[i],
            device_id={"seg": target}, device_id_type=MESH)

    for load in loads[4:]:
        load.wait()
    gates_ref[0:1, :] = fraction_ref[...]
    gates_ref[1:2, :] = shift_ref[...].astype(f32)
    gates_ref[2:8, :] = jnp.zeros((6, pulse_count), f32)
    gcols[...] = gates_ref[...].T
    lane = lax.broadcasted_iota(jnp.int32, (ROWS, gates), 1)

    def migrate_rows(q, carry):
        rows = pl.ds(pl.multiple_of(q * ROWS, ROWS), ROWS)
        frac = gcols[rows, 0:1]
        shift = gcols[rows, 1:2].astype(jnp.int32)
        for c in range(2):
            x = pulses_ref[c, rows, :].astype(jnp.float32)
            nxt = jnp.where(lane == gates - 1, 0.0, pltpu.roll(x, gates - 1, 1))
            z = (1.0 - frac) * x + frac * nxt
            for b in range(SHIFT_BITS):
                z = jnp.where((shift & (1 << b)) != 0, pltpu.roll(z, gates - (1 << b), 1), z)
            z = jnp.where(lane + shift < gates, z, 0.0)
            mig[rows, c * gates:(c + 1) * gates] = z.astype(jnp.bfloat16)
        return carry

    chunks = pulse_count // ROWS
    lax.fori_loop(0, chunks // 2, migrate_rows, 0, unroll=4)
    pl.semaphore_wait(barrier, jnp.minimum(me, REACH) + jnp.minimum(n - 1 - me, REACH))
    each(lambda i, peer: params_copy(2 * REACH - i, peer).start())
    lax.fori_loop(chunks // 2, chunks, migrate_rows, 0, unroll=4)

    pulse = (me * pulse_count + lax.broadcasted_iota(jnp.int32, (ROWS, pulse_count), 1)).astype(jnp.float32)

    def term(packed):
        cols[...] = packed.T

        def weigh(q, carry):
            rows = pl.ds(pl.multiple_of(q * ROWS, ROWS), ROWS)
            low = pl.ds(pl.multiple_of(waves + q * ROWS, ROWS), ROWS)
            center, start, end = cols[rows, 0:1], cols[rows, 1:2], cols[rows, 2:3]
            rate, slope, amp = cols[rows, 3:4], cols[rows, 4:5], cols[rows, 5:6]
            r = (pulse - center) * scale
            t = r * (rate * r + slope)
            t = t - jnp.floor(t + 0.5)
            u = t * t
            s = t * horner(SIN, u)
            c = horner(COS, u)
            a = jnp.where((pulse >= start) & (pulse < end), amp, 0.0)
            twice = (a + a) * s
            wts[rows, :] = (a - twice * s).astype(jnp.bfloat16)
            wts[low, :] = (twice * c).astype(jnp.bfloat16)
            return carry

        lax.fori_loop(0, waves // ROWS, weigh, 0, unroll=True)
        real = jnp.dot(wts[...], mig[:, :gates], preferred_element_type=jnp.float32)
        imag = jnp.dot(wts[...], mig[:, gates:], preferred_element_type=jnp.float32)
        return real[:waves] - imag[waves:], imag[:waves] + real[waves:]

    def term_for(o):
        i = o + REACH
        params_copy(i, me + o).wait_recv()
        return term(pbuf[i])

    def own(k):
        return 4 - 2 * k - 2 * lax.div(k, 2)

    def help_copy(k):
        return pltpu.make_async_remote_copy(
            src_ref=helpb.at[k], dst_ref=gotb.at[k], send_sem=gsend.at[k], recv_sem=grecv.at[k],
            device_id={"seg": mate}, device_id_type=MESH)

    def sum_copy(k, target):
        return pltpu.make_async_remote_copy(
            src_ref=sendb.at[k], dst_ref=recvb.at[k], send_sem=tsend.at[k], recv_sem=trecv.at[k],
            device_id={"seg": target}, device_id_type=MESH)

    def alone(k):
        @pl.when(exists(me + way * own(k)))
        def _():
            real, imag = term_for(way * own(k))
            sendb[k, 0] = real.astype(jnp.bfloat16)
            sendb[k, 1] = imag.astype(jnp.bfloat16)
            sum_copy(k, me + way * own(k)).start()

    def assist(k):
        o = way * (1 - own(k))

        @pl.when(exists(me + o))
        def _():
            real, imag = term_for(o)
            helpb[k, 0] = real.astype(jnp.bfloat16)
            helpb[k, 1] = imag.astype(jnp.bfloat16)
            help_copy(k).start()

    def shared(k):
        @pl.when(exists(me + way * own(k)))
        def _():
            real, imag = term_for(way * own(k))
            help_copy(k).wait_recv()
            sendb[k, 0] = (real + gotb[k, 0].astype(f32)).astype(jnp.bfloat16)
            sendb[k, 1] = (imag + gotb[k, 1].astype(f32)).astype(jnp.bfloat16)
            sum_copy(k, me + way * own(k)).start()

    loop(1, lambda k: alone(k + 3))
    loop(3, assist)
    loop(3, shared)
    real, imag = term_for(way)
    helpb[3, 0] = real.astype(jnp.bfloat16)
    helpb[3, 1] = imag.astype(jnp.bfloat16)
    help_copy(3).start()
    real, imag = term(params_ref[...])
    help_copy(3).wait_recv()
    acc[0] = real + gotb[3, 0].astype(f32)
    acc[1] = imag + gotb[3, 1].astype(f32)

    def take(j):
        k = 3 - j

        @pl.when(exists(me - way * own(k)))
        def _():
            sum_copy(k, me - way * own(k)).wait_recv()
            acc[0] += recvb[k, 0].astype(f32)
            acc[1] += recvb[k, 1].astype(f32)

    loop(4, take)
    power[LOOK:LOOK + waves, :] = acc[0] * acc[0] + acc[1] * acc[1]

    def halo_copy(side):
        low = LOOK if side == 0 else waves
        into = LOOK + waves if side == 0 else 0
        target = me - 1 if side == 0 else me + 1
        return pltpu.make_async_remote_copy(
            src_ref=power.at[pl.ds(low, LOOK)], dst_ref=power.at[pl.ds(into, LOOK)],
            send_sem=hsend.at[side], recv_sem=hrecv.at[side],
            device_id={"seg": target}, device_id_type=MESH)

    @pl.when(me > 0)
    def _():
        halo_copy(0).start()

    @pl.when(me < n - 1)
    def _():
        halo_copy(1).start()

    @pl.when(me == 0)
    def _():
        power[0:LOOK, :] = jnp.zeros((LOOK, gates), jnp.float32)

    @pl.when(me == n - 1)
    def _():
        power[LOOK + waves:, :] = jnp.zeros((LOOK, gates), jnp.float32)

    focus_ref[...] = acc[...].astype(jnp.bfloat16)

    def average(low, count):
        size = count + 2 * LOOK
        total = power[low:low + size, :]
        last = total[2 * LOOK:]
        step = 1
        while step < 2 * LOOK:
            size -= step
            total = total[:size] + total[step:step + size]
            step *= 2
        look_ref[low:low + count, :] = (total[:count] + last) * (1.0 / float(2 * LOOK + 1))

    average(LOOK, waves - 2 * LOOK)
    each(lambda i, peer: params_copy(2 * REACH - i, peer).wait_send())

    def drain(k):
        @pl.when(exists(me + way * own(k)))
        def _():
            sum_copy(k, me + way * own(k)).wait_send()

    loop(4, drain)

    def drain_help(k):
        @pl.when(exists(me + way * (1 - own(k))))
        def _():
            help_copy(k).wait_send()

    loop(3, drain_help)
    help_copy(3).wait_send()

    @pl.when(me > 0)
    def _():
        halo_copy(0).wait_send()
        halo_copy(1).wait_recv()

    @pl.when(me < n - 1)
    def _():
        halo_copy(1).wait_send()
        halo_copy(0).wait_recv()

    average(0, LOOK)
    average(waves - LOOK, LOOK)


def hand_over(focus_in, look_in, focus_out, look_out, focus, look, sems):
    arrays = ((focus_in, focus, focus_out), (look_in, look, look_out))
    loads = [pltpu.make_async_copy(a, b, sems.at[i]) for i, (a, b, _) in enumerate(arrays)]
    stores = [pltpu.make_async_copy(b, c, sems.at[2 + i]) for i, (_, b, c) in enumerate(arrays)]
    for load in loads:
        load.start()
    for load, store in zip(loads, stores):
        load.wait()
        store.start()
    for store in stores:
        store.wait()


def shards(pulses, fraction, gate_shift, aperture_start, aperture_end, doppler, chirp_rate):
    n = lax.axis_size("seg")
    pulse_count, gates = pulses.shape[1:]
    waves = aperture_start.shape[0]
    f32 = jnp.float32
    vmem = pl.BlockSpec(memory_space=pltpu.VMEM)
    hbm = pl.BlockSpec(memory_space=pltpu.HBM)
    slots = 2 * REACH + 1
    dma = pltpu.SemaphoreType.DMA
    block = pltpu.VMEM((4, 2, waves, gates), jnp.bfloat16)
    rows = [a.reshape(1, -1) for a in (
        fraction, gate_shift, aperture_start, aperture_end, doppler, chirp_rate)]
    outs = (jax.ShapeDtypeStruct((2, waves, gates), jnp.bfloat16), jax.ShapeDtypeStruct((waves, gates), f32))
    results = pl.pallas_call(
        functools.partial(kernel, n),
        out_shape=outs,
        in_specs=[hbm] * 7,
        out_specs=(vmem, vmem),
        scratch_shapes=[pltpu.VMEM(pulses.shape, pulses.dtype)] + [pltpu.VMEM(a.shape, a.dtype) for a in rows] + [
            pltpu.VMEM((8, waves), f32),
            pltpu.VMEM((8, pulse_count), f32),
            pltpu.VMEM((pulse_count, 2 * gates), jnp.bfloat16),
            pltpu.VMEM((2 * waves, pulse_count), jnp.bfloat16),
            pltpu.VMEM((waves, 8), f32),
            pltpu.VMEM((pulse_count, 8), f32),
            pltpu.VMEM((slots, 8, waves), f32),
            block, block, block, block,
            pltpu.VMEM((2, waves, gates), f32),
            pltpu.VMEM((waves + 2 * LOOK, gates), f32),
            dma((7,)), dma((slots,)), dma((slots,)), dma((4,)), dma((4,)), dma((4,)), dma((4,)), dma((2,)), dma((2,)),
        ],
        compiler_params=pltpu.CompilerParams(
            collective_id=0, has_side_effects=True, vmem_limit_bytes=60 * 1024 * 1024),
    )(pulses, *rows)
    return pl.pallas_call(
        hand_over, out_shape=outs, in_specs=[hbm, hbm], out_specs=(hbm, hbm),
        scratch_shapes=[pltpu.VMEM(o.shape, o.dtype) for o in outs] + [dma((4,))],
        compiler_params=pltpu.CompilerParams(vmem_limit_bytes=60 * 1024 * 1024),
    )(*results)


def solution(mesh):
    seg = P(("arcs", "seg"))
    return jax.shard_map(
        shards,
        mesh=mesh,
        in_specs=(P(None, ("arcs", "seg"), None), seg, seg, seg, seg, seg, seg),
        out_specs=(P(None, ("arcs", "seg"), None), P(("arcs", "seg"), None)),
        check_vma=False,
    )
```
